128 devices in a mesh: frame: 8 (over y, core), refl: 16 (over x, z).
Axes of the slice: x: 4, y: 4, z: 4, core: 2. Of those that a mesh axis runs over, the one named last changes fastest.
Arguments:
- image: float32 [64, 512, 512], P('frame', 'refl'), may hold values from 0.5 to 160
- gain: float32 [512, 512], P('refl'), may hold values from 0.5 to 1.5
- pixel_mask: int32 [512, 512], P('refl'), may hold values 0 or 1
- anchor_row: int32 [16384], P(('frame', 'refl')), may hold values from 0 to 16
- anchor_col: int32 [16384], P(('frame', 'refl')), may hold values from 0 to 496
- owner: int32 [16384, 1], P(('frame', 'refl')), may hold values from 0 to 127; in each aligned block of 128 rows (0 to 127, 128 to 255, ...) at most 2 rows name the same one
- region: int32 [16384, 1], P(('frame', 'refl')), may hold values from 0 to 31
Outputs:
- strong: bfloat16 [64, 512, 512], P('frame', 'refl')
- intensity: float32 [128, 256], P(('frame', 'refl'))
- profiles: float32 [32, 729], replicated
The draws below stay inside these ranges and needn't reach their ends.
Inputs may be any that keep to these rules, and one draw needn't show every extreme that they name: Among the 128 reflections of one source (aligned blocks of 128 rows) at most 2 name the same owner, a bound that some block reaches. Every region is named by some reflection.
All inputs are finite; a program needn't handle non-finite values. No bound on the sum of `pixel_mask` on one device may be relied on, other than what follows from the above.
Results may differ from the reference program's by a relative error of at most 0.006.
Values may be sent and summed in bfloat16 or wider, within the bound.
No kernel may reach another device: no remote copies, remote signals or barrier semaphores. Data moves between devices by JAX's collectives and lax.ppermute only.
A program may use at most 128 MiB of HBM per device.

```python
import math
import jax
import jax.numpy as jnp
import numpy as np
from jax import lax

FR_DEV = 8
R_DEV = 32
NCOLS = 512
K = 128
SB_EDGE = 16
GRID = 9
REGIONS = 32
ITERS = 3
FRAMES = 64
NROWS = 512
CAP = 2
REFLS = 16384
N_FRAME = 8
N_REFL = 16


def draw_image(key, part):
    key = jax.random.fold_in(key, 11)
    level_key, noise_key, seed_key, spot_key = jax.random.split(key, 4)
    shape_full = (FRAMES, NROWS, NCOLS)
    tile_rows = (NROWS + 7) // 8
    tile_cols = (NCOLS + 31) // 32
    level_high = 16.0
    coarse_levels = jnp.exp(jax.random.uniform(level_key, (tile_rows, tile_cols), jnp.float32, 0.0, jnp.log(level_high)))
    row_index = jnp.arange(NROWS, dtype=jnp.int32) // 8
    col_index = jnp.arange(NCOLS, dtype=jnp.int32) // 32
    levels_map = coarse_levels[row_index][:, col_index]
    noise_values = jax.random.normal(noise_key, shape_full, jnp.float32)
    seed_mask = jax.random.uniform(seed_key, shape_full, jnp.float32) < 1.0 / 384.0
    spot_scale = jnp.exp(jax.random.uniform(spot_key, shape_full, jnp.float32, jnp.log(6.0), jnp.log(20.0)))
    spot_amplitude = jnp.where(seed_mask, spot_scale, 0.0) * jnp.sqrt(levels_map + 1.0)[None]
    padded_spots = jnp.pad(spot_amplitude, ((0, 0), (1, 1), (1, 1)))
    blob_sum = jnp.zeros(shape_full, jnp.float32)
    for row_step in range(3):
        for col_step in range(3):
            blob_sum = blob_sum + padded_spots[:, row_step:row_step + NROWS, col_step:col_step + NCOLS]
    counts_value = levels_map[None] + jnp.sqrt(levels_map)[None] * noise_values + blob_sum
    return jnp.clip(counts_value, 0.5, 160.0)


def plant(values, rng, low, top_value):
    extent = values.shape
    spot = [jax.random.randint(jax.random.fold_in(rng, axis), (), 0, extent[axis]) for axis in range(len(extent))]
    values = values.at[tuple(spot)].set(low)
    longest = extent.index(max(extent))
    spot[longest] = (spot[longest] + 1) % extent[longest]
    return values.at[tuple(spot)].set(top_value)


def different_ones(own_key, rows, amount, top, lift):
    order = jax.random.permutation(jax.random.fold_in(own_key, 1), amount)
    boost = order
    for power in range(3):
        boost = boost * boost // amount
    boost = boost * lift // amount
    tickets = jax.random.randint(jax.random.fold_in(own_key, 2), (rows, amount), 0, 4096) + boost
    fixed_rows = jax.random.permutation(jax.random.fold_in(own_key, 3), rows)[jnp.arange(amount) % rows]
    tickets = jnp.where(jnp.arange(rows)[:, None] == fixed_rows[None, :], 1 << 14, tickets)
    priority = tickets * amount + jnp.arange(amount)
    return lax.top_k(priority.astype(jnp.int32), top)[1].astype(jnp.int32)


def routed_block(key, own, number, rows, count, top, limit, slope):
    order = jax.random.permutation(key, count)
    heavy_load, ordinary = portions_of(count, rows * top, limit, slope, True), portions_of(count, rows * top, limit, slope, False)
    places = jnp.arange(count)

    def named(tallies, rotation):
        used = int((tallies > 0).sum())
        fixed = max(1, used // 4)
        passed = fixed + (places - fixed + rotation * (used - fixed)) % max(1, count - fixed)
        return jnp.zeros((count,), jnp.int32).at[order[jnp.where(places < fixed, places, passed)]].set(jnp.asarray(tallies, jnp.int32))

    tallies = jnp.where(number % 4 == 0, named(heavy_load, number // 4), named(ordinary, number - number // 4 - 1))
    mixed = jax.random.permutation(jax.random.fold_in(own, 3), count)
    donor, sink = mixed[0:count // 2 * 2:2], mixed[1:count // 2 * 2:2]
    margin = jnp.minimum(tallies[donor] - 1, limit - tallies[sink]) // 2
    margin = jnp.where((donor == order[0]) | (sink == order[0]) | (tallies[sink] == 0), 0, jnp.maximum(margin, 0))
    passed = jax.random.randint(jax.random.fold_in(own, 4), (count // 2,), 0, 1 << 20) % (margin + 1)
    tallies = tallies.at[donor].add(-passed).at[sink].add(passed)
    items = jnp.searchsorted(jnp.cumsum(tallies), jnp.arange(rows * top), side="right").astype(jnp.int32)
    listing = items.reshape(top, rows).T
    listing = listing[jax.random.permutation(jax.random.fold_in(own, 1), rows)]
    rotation = jax.random.randint(jax.random.fold_in(own, 2), (rows, 1), 0, top)
    return jnp.take_along_axis(listing, (jnp.arange(top)[None, :] + rotation) % top, axis=1)


def portions_of(number_of, total, limit, lean, full):
    portions = [(1 << 20) // math.isqrt(grade ** lean) + 1 for grade in range(1, number_of + 1)]
    largest = limit if full else min(limit, max(-(-total // number_of), total * portions[0] // sum(portions)))
    least = 1 if total - largest >= number_of - 1 else 0
    counts, rest = [largest] + [least] * (number_of - 1), total - largest - least * (number_of - 1)
    while rest > 0:
        candidates = [i for i in range(1, number_of) if counts[i] < largest] or [i for i in range(1, number_of) if counts[i] < limit]
        pool, remaining = sum([portions[i] for i in candidates]), rest
        for i in candidates:
            addition = min(limit - counts[i], max(1, remaining * portions[i] // pool), rest)
            counts[i] = counts[i] + addition
            rest = rest - addition
    return np.array(counts)


def setup_inputs(seed: int = 0) -> dict:
    keys = jax.random.split(jax.random.key(seed), 8)
    image = draw_image(jax.random.fold_in(keys[7], 71), 0)
    gain = jnp.clip(1.0 + 0.1 * jax.random.normal(keys[1], (NROWS, NCOLS), jnp.float32), 0.5, 1.5)
    pixel_mask = plant((jax.random.randint(keys[2], (NROWS, NCOLS), 0, 16) < 15).astype(jnp.int32), jax.random.fold_in(keys[2], 1), 0, 1)
    anchor_row = plant(jax.random.randint(keys[3], (REFLS,), 0, R_DEV - SB_EDGE + 1), jax.random.fold_in(keys[3], 1), 0, R_DEV - SB_EDGE).astype(jnp.int32)
    anchor_col = plant(jax.random.randint(keys[4], (REFLS,), 0, NCOLS - SB_EDGE + 1), jax.random.fold_in(keys[4], 1), 0, NCOLS - SB_EDGE).astype(jnp.int32)
    owner_keys = jax.random.split(jax.random.fold_in(keys[5], 1), REFLS // K)
    owner_turns = jax.random.permutation(jax.random.fold_in(keys[5], 3), REFLS // K)
    owner = jax.vmap(lambda own, number: routed_block(jax.random.fold_in(keys[5], 2), own, number, K, N_FRAME * N_REFL, 1, CAP, 2))(owner_keys, owner_turns).reshape((REFLS, 1))
    region = different_ones(keys[6], REFLS, REGIONS, 1, 0)
    return dict(image=image, gain=gain, pixel_mask=pixel_mask, anchor_row=anchor_row, anchor_col=anchor_col, owner=owner, region=region)


def tent_table():
    centres = (jnp.arange(SB_EDGE, dtype=jnp.float32) + 0.5) * (GRID / SB_EDGE)
    grid_bins = jnp.arange(GRID, dtype=jnp.float32) + 0.5
    return jnp.maximum(0.0, 1.0 - jnp.abs(centres[None, :] - grid_bins[:, None]))

def box_sum(padded, height, columns):
    along_rows = padded[..., 0:height, :]
    for offset in range(1, 7):
        along_rows = along_rows + padded[..., offset:offset + height, :]
    result = along_rows[..., 0:columns]
    for offset in range(1, 7):
        result = result + along_rows[..., offset:offset + columns]
    return result

def dispersion_weights(corrected, mask_float, padded):
    height = corrected.shape[-2]
    columns = corrected.shape[-1]
    stacked = jnp.stack([padded[0], padded[1], padded[0] * padded[0]])
    box_sums = box_sum(stacked, height, columns)
    box_total = box_sums[0]
    box_count = box_sums[1]
    box_square = box_sums[2]
    background = box_total / jnp.maximum(box_count, 1.0)
    variance = (box_square - box_total * background) / jnp.maximum(box_count - 1.0, 1.0)
    dispersion = variance / (background + 1.0)
    threshold = 1.0 + 6.0 * jnp.sqrt(2.0 / jnp.maximum(box_count - 1.0, 1.0))
    spread_gate = jax.nn.sigmoid(2.0 * (dispersion - threshold))
    peak_gate = jax.nn.sigmoid((corrected - background - 3.0 * jnp.sqrt(background)) / jnp.sqrt(background + 1.0))
    return (mask_float * spread_gate * peak_gate, background)

def weighted_fields(shoebox_parts):
    values = shoebox_parts.astype(jnp.float32)
    return jnp.stack([values[:, 0], values[:, 1], values[:, 2] * values[:, 0]], axis=1)

def to_grid(fields, depth_table, grid_table):
    grid_values = jnp.einsum('nfzyx,az,by,cx->nfabc', fields, depth_table, grid_table, grid_table, precision=lax.Precision.HIGHEST)
    return grid_values.reshape(fields.shape[0], 3, GRID * GRID * GRID)

def profile_fit(count_grid, back_grid, profile):
    signal = count_grid - back_grid
    estimate = lax.optimization_barrier(jnp.sum(signal, axis=1, keepdims=True))
    for iteration in range(ITERS):
        weight_var = back_grid + jnp.maximum(estimate, 0.0) * profile + 1.0
        upper_sum = lax.optimization_barrier(jnp.sum(profile * signal / weight_var, axis=1, keepdims=True))
        lower_sum = lax.optimization_barrier(jnp.sum(profile * profile / weight_var, axis=1, keepdims=True))
        estimate = upper_sum / lower_sum
    return estimate[:, 0]

def reference(image, gain, pixel_mask, anchor_row, anchor_col, owner, region):
    mask_float = pixel_mask.astype(jnp.float32)

    def per_frame(detector_frame):
        corrected = detector_frame * gain * mask_float
        padded = jnp.pad(jnp.stack([corrected, mask_float]), ((0, 0), (3, 3), (3, 3)))
        strong, background = dispersion_weights(corrected, mask_float, padded)
        return (corrected.astype(jnp.bfloat16), background.astype(jnp.bfloat16), strong.astype(jnp.bfloat16))
    counts_b, back_b, strong_b = lax.map(per_frame, image)
    fields = jnp.stack([counts_b, back_b, strong_b])
    fields = jnp.pad(fields, ((0, 0), (0, FR_DEV), (0, 0), (0, 0)))
    grid_table = tent_table()
    devices = N_FRAME * N_REFL
    source = jnp.arange(REFLS, dtype=jnp.int32) // K
    start_frame = source // N_REFL * FR_DEV
    start_row = source % N_REFL * R_DEV + anchor_row
    anchor_zero = jnp.zeros((), jnp.int32)

    def extract(frame_start, row_start, col_start):
        return lax.dynamic_slice(fields, (anchor_zero, frame_start, row_start, col_start), (3, 2 * FR_DEV, SB_EDGE, SB_EDGE))

    def per_source(starts):
        shoebox_parts = jax.vmap(extract)(starts[0], starts[1], starts[2])
        return to_grid(weighted_fields(shoebox_parts), grid_table, grid_table)
    grid_values = lax.map(per_source, (start_frame.reshape(devices, K), start_row.reshape(devices, K), anchor_col.reshape(devices, K)))
    grid_values = grid_values.reshape(REFLS, 3, GRID * GRID * GRID)
    count_grid = grid_values[:, 0]
    back_grid = grid_values[:, 1]
    strong_grid = grid_values[:, 2]
    contribution = strong_grid / lax.optimization_barrier(jnp.sum(count_grid, axis=1, keepdims=True))
    regions = region[:, 0]
    profile_sum = jax.ops.segment_sum(contribution, regions, num_segments=REGIONS)
    profiles = profile_sum / lax.optimization_barrier(jnp.sum(profile_sum, axis=1, keepdims=True))
    fitted = profile_fit(count_grid, back_grid, profiles[regions])
    owners = owner[:, 0].reshape(devices, K)
    same_owner = owners[:, :, None] == owners[:, None, :]
    position = jnp.arange(K, dtype=jnp.int32)
    earlier = position[None, :] < position[:, None]
    slot_rank = lax.optimization_barrier(jnp.sum(jnp.where(same_owner & earlier[None], 1, 0), axis=2)).astype(jnp.int32)
    column = (jnp.arange(devices, dtype=jnp.int32)[:, None] * CAP + slot_rank).reshape(REFLS)
    intensity = jnp.zeros((devices, devices * CAP), jnp.float32).at[owner[:, 0], column].set(fitted)
    return (strong_b, intensity, profiles)
```

```python
import functools

import jax
import jax.numpy as jnp
import numpy as np
from jax import lax
from jax.experimental import pallas as pl
from jax.experimental.pallas import tpu as pltpu
from jax.sharding import PartitionSpec as P

SB_EDGE = 16
GRID = 9
REGIONS = 32
ITERS = 3
HALO = 3
LANES = 128
HALF_BINS = 5
PLANE = 88
HALF_ROWS = HALF_BINS * PLANE
FULL_ROWS = GRID * PLANE
WIDE_ROWS = 896
PARAMS = pltpu.CompilerParams(vmem_limit_bytes=48 * 1024 * 1024)


def tent_values():
    centres = (np.arange(SB_EDGE, dtype=np.float32) + 0.5) * (GRID / SB_EDGE)
    bins = np.arange(GRID, dtype=np.float32) + 0.5
    return np.maximum(0.0, 1.0 - np.abs(centres[None, :] - bins[:, None]))


TENT = tent_values()
EDGE_WEIGHT = TENT.sum(axis=0)


def depth_mixer(rows, frames):
    mixer = np.zeros((2, rows, 8, rows, frames), np.float32)
    for row in range(rows):
        mixer[0, row, :HALF_BINS, row, :] = TENT[:HALF_BINS, :frames]
        mixer[1, row, :HALF_BINS, row, :] = TENT[GRID - HALF_BINS :, frames:]
    return mixer.reshape(2 * rows * 8, rows * frames)


def dot(a, b):
    return lax.dot_general(a, b, (((1,), (0,)), ((), ())), preferred_element_type=jnp.float32)


def dot_nt(a, b):
    return lax.dot_general(a, b, (((1,), (1,)), ((), ())), preferred_element_type=jnp.float32)


def split_two(x):
    high = x.astype(jnp.bfloat16)
    return high, (x - high.astype(jnp.float32)).astype(jnp.bfloat16)


def edge_kernel(place, top, bottom, gain, mask, first, second):
    height = gain.shape[0]
    odd = place[0] == 1

    def edge(block, local, start):
        parts = []
        for k in range(HALO):
            row = start + k
            mask_row = mask[row : row + 1, :].astype(jnp.float32)
            parts.append(block[:, local + k, :] * (gain[row : row + 1, :] * mask_row))
        return parts, mask[start : start + HALO, :].astype(jnp.float32)

    head, head_mask = edge(top, 0, 0)
    tail, tail_mask = edge(bottom, 8 - HALO, height - HALO)
    for k in range(HALO):
        first[k] = jnp.where(odd, head[k], tail[k])
        second[k] = jnp.where(odd, tail[k], head[k])
    first[HALO] = jnp.zeros(first.shape[1:], jnp.float32)
    second[HALO] = jnp.zeros(second.shape[1:], jnp.float32)
    first[HALO, 0:HALO] = jnp.where(odd, head_mask, tail_mask)
    second[HALO, 0:HALO] = jnp.where(odd, tail_mask, head_mask)


def shoebox_offsets(anchors, extent):
    return lax.broadcasted_iota(jnp.int32, (extent, LANES), 0) - anchors


def total_weights(anchors, extent):
    offset = shoebox_offsets(anchors, extent)
    inside = (offset >= 0) & (offset < SB_EDGE)
    border = (offset == 0) | (offset == SB_EDGE - 1)
    return jnp.where(border, float(EDGE_WEIGHT[0]), jnp.where(inside, 1.0, 0.0))


def level_kernel(place, image, gain, mask, own, from_core, from_chip, corrected, totals):
    frames, height, columns = image.shape
    odd = place[1] == 1
    scale = gain[...] * mask[...].astype(jnp.float32)
    values = image[...] * scale[None]
    corrected[...] = jnp.transpose(values, (1, 0, 2))
    counts = values.astype(jnp.bfloat16).astype(jnp.float32)
    inner = counts[1]
    for z in range(2, frames - 1):
        inner = inner + counts[z]
    border = float(EDGE_WEIGHT[0])
    lower = inner + counts[frames - 1] + border * counts[0]
    upper = inner + counts[0] + border * counts[frames - 1]
    partner = jnp.where(odd, from_core[...], from_chip[...])
    for half, (levels, anchors) in enumerate(((lower, own[...]), (upper, partner))):
        high, low = split_two(levels)
        by_column = total_weights(anchors[1:2], columns).astype(jnp.bfloat16)
        by_row = total_weights(anchors[0:1], height)
        sums = dot(high, by_column) + dot(low, by_column)
        totals[half : half + 1, :] = jnp.sum(sums * by_row, axis=0, keepdims=True)


def window_sums(x):
    width = x.shape[-1]
    axis = x.ndim - 1
    pairs = x + pltpu.roll(x, 1, axis)
    fours = pairs + pltpu.roll(pairs, 2, axis)
    return fours + pltpu.roll(fours, width - 3, axis) - x


def spot_kernel(
    place,
    corrected,
    mask,
    halo_first,
    halo_second,
    own,
    from_core,
    from_chip,
    totals,
    totals_core,
    totals_chip,
    mixer,
    strong,
    lower_grids,
    upper_grids,
    partial,
    padded,
    mask_rows,
    count_terms,
    strong_rows,
    fields,
    column_tents,
    spread,
    packed,
    contributions,
):
    height, frames, columns = corrected.shape
    odd_band = place[0] == 1
    odd_slab = place[1] == 1
    has_partner = place[2] == 1
    zero_tail = jnp.zeros((height, LANES), jnp.float32)

    halo_a = halo_first[...]
    halo_b = halo_second[...]
    before = jnp.where(odd_band, halo_a, halo_b)
    after = jnp.where(odd_band, halo_b, halo_a)
    padded[0:HALO] = before[0:HALO]
    padded[HALO : HALO + height] = corrected[...]
    padded[HALO + height :] = after[0:HALO]

    mask_rows[8 - HALO : 8, :] = before[HALO, 0:HALO]
    mask_rows[8 : 8 + height, :] = mask[...].astype(jnp.float32)
    mask_rows[8 + height : 8 + height + HALO, :] = after[HALO, 0:HALO]
    count = mask_rows[8 - HALO : 8 - HALO + height, :]
    for k in range(1, 2 * HALO + 1):
        count = count + mask_rows[8 - HALO + k : 8 - HALO + k + height, :]
    count = window_sums(jnp.concatenate([count, zero_tail], axis=1))[:, 0:columns]
    per_spread = 1.0 / jnp.maximum(count - 1.0, 1.0)
    count_terms[0] = 1.0 / jnp.maximum(count, 1.0)
    count_terms[1] = per_spread
    count_terms[2] = 1.0 + 6.0 * jnp.sqrt(2.0 * per_spread)

    frame_tail = jnp.zeros((2, frames, LANES), jnp.float32)

    def row_pair(i, carry):
        r = 2 * i
        rows = [padded[r + k] for k in range(2 * HALO + 2)]
        shared = rows[1]
        for k in range(2, 2 * HALO + 1):
            shared = shared + rows[k]
        squares = [x * x for x in rows]
        shared_square = squares[1]
        for k in range(2, 2 * HALO + 1):
            shared_square = shared_square + squares[k]
        total = jnp.stack([shared + rows[0], shared + rows[-1]])
        square = jnp.stack([shared_square + squares[0], shared_square + squares[-1]])
        total = window_sums(jnp.concatenate([total, frame_tail], axis=2))[:, :, 0:columns]
        square = window_sums(jnp.concatenate([square, frame_tail], axis=2))[:, :, 0:columns]
        value = jnp.stack([rows[HALO], rows[HALO + 1]])

        def term(j):
            return jnp.stack(
                [jnp.broadcast_to(count_terms[j, pl.ds(r + k, 1), :], (frames, columns)) for k in range(2)]
            )

        live = jnp.stack(
            [jnp.broadcast_to(mask_rows[pl.ds(8 + r + k, 1), :], (frames, columns)) for k in range(2)]
        )
        background = total * term(0)
        variance = (square - total * background) * term(1)
        per_root = lax.rsqrt(background + 1.0)
        excess = 2.0 * (variance * (per_root * per_root) - term(2))
        peak = (value - background - 3.0 * jnp.sqrt(background)) * per_root
        weight = live / ((1.0 + jnp.exp(-excess)) * (1.0 + jnp.exp(-peak)))
        weight_b = weight.astype(jnp.bfloat16).astype(jnp.float32)
        value_b = value.astype(jnp.bfloat16).astype(jnp.float32)
        background_b = background.astype(jnp.bfloat16).astype(jnp.float32)
        strong_rows[pl.ds(r, 2)] = weight_b
        at = pl.ds(pl.multiple_of(r * frames, 2 * frames), 2 * frames)
        flat = (2 * frames, columns)
        fields[0, at, :] = (value_b - background_b).reshape(flat).astype(jnp.bfloat16)
        fields[1, at, :] = background_b.reshape(flat).astype(jnp.bfloat16)
        fields[2, at, :] = (weight_b * value_b).reshape(flat).astype(jnp.bfloat16)
        return carry

    lax.fori_loop(0, height // 2, row_pair, 0)
    strong[...] = jnp.transpose(strong_rows[...], (1, 0, 2)).astype(jnp.bfloat16)

    partner = jnp.where(odd_slab, from_core[...], from_chip[...])
    own_info = own[...]
    infos = (own_info, partner)
    for half, info in enumerate(infos):
        offset = shoebox_offsets(info[1:2], columns)
        centre = (offset.astype(jnp.float32) + 0.5) * (GRID / SB_EDGE)
        for c in range(GRID):
            tent = jnp.maximum(1.0 - jnp.abs(centre - (c + 0.5)), 0.0)
            if c == 0:
                tent = jnp.where(offset >= 0, tent, 0.0)
            if c == GRID - 1:
                tent = jnp.where(offset < SB_EDGE, tent, 0.0)
            column_tents[half, :, c * LANES : (c + 1) * LANES] = tent.astype(jnp.bfloat16)

    contributions[...] = jnp.zeros(contributions.shape, jnp.float32)
    packed[GRID * GRID * 8 :, :] = jnp.zeros((PLANE * 8 - GRID * GRID * 8, LANES), jnp.float32)
    partner_total = jnp.where(odd_slab, totals_core[0:1], totals_chip[0:1]) + totals[1:2]
    partner_total = jnp.where(has_partner, partner_total, 1.0)
    own_total = totals[0:1] + jnp.where(odd_slab, totals_chip[1:2], totals_core[1:2])
    per_total = (1.0 / own_total, 1.0 / partner_total)
    mixed_rows = height * 8

    for field in range(3):
        mixed = dot(mixer[...], fields[field]).astype(jnp.bfloat16)
        for half in range(2):
            shift = jnp.broadcast_to(infos[half][0:1], (8, LANES))
            spread[...] = dot(mixed[half * mixed_rows : (half + 1) * mixed_rows], column_tents[half])
            bits = [(shift & (1 << k)) != 0 for k in range(5)]

            def one_column(c, carry):
                at = pl.ds(pl.multiple_of(c * LANES, LANES), LANES)
                rows = [spread[8 * r : 8 * r + 8, at] for r in range(height)]
                rows = [
                    jnp.where(bits[4], rows[r + 16], rows[r]) if r + 16 < height else rows[r]
                    for r in range(31)
                ]
                for k in (3, 2, 1, 0):
                    keep = 16 + (1 << k) - 1
                    rows = [jnp.where(bits[k], rows[r + (1 << k)], rows[r]) for r in range(keep)]
                for b in range(GRID):
                    value = None
                    for y in range(SB_EDGE):
                        if TENT[b, y] != 0.0:
                            term = rows[y] * float(TENT[b, y])
                            value = term if value is None else value + term
                    packed[pl.ds(pl.multiple_of((b * GRID + c) * 8, 8), 8), :] = value
                return carry

            lax.fori_loop(0, GRID, one_column, 0)
            for a in range(HALF_BINS):
                plane = packed[pl.ds(a, PLANE, stride=8), :]
                at = slice(a * PLANE, (a + 1) * PLANE)
                if field == 2:
                    first = at.start + half * (FULL_ROWS - HALF_ROWS)
                    contributions[first : first + PLANE, half * LANES : (half + 1) * LANES] = (
                        plane * per_total[half]
                    )
                elif half == 0:
                    lower_grids[field, at, :] = plane
                else:
                    upper_grids[field, at, :] = plane

    regions = lax.broadcasted_iota(jnp.int32, (REGIONS, LANES), 0)
    own_member = jnp.where(regions == own_info[2:3], 1.0, 0.0)
    partner_member = jnp.where((regions == partner[2:3]) & has_partner, 1.0, 0.0)
    members = jnp.concatenate([own_member, partner_member], axis=1).astype(jnp.bfloat16)
    high, low = split_two(contributions[...])
    partial[...] = dot_nt(members, high) + dot_nt(members, low)


def fit_kernel(place, sums, own, slots, lower_grids, upper_core, upper_chip, profiles, estimates, signal, back, chosen):
    odd_slab = place[1] == 1
    total = jnp.sum(sums[...], axis=1, keepdims=True)
    profile = sums[...] / total
    profiles[...] = jnp.concatenate(
        [profile[:, a * PLANE : a * PLANE + GRID * GRID] for a in range(GRID)], axis=1
    )
    regions = lax.broadcasted_iota(jnp.int32, (REGIONS, LANES), 0)
    member = jnp.where(regions == own[2:3], 1.0, 0.0)
    chosen[...] = lax.dot_general(
        jnp.transpose(profile, (1, 0))[0:FULL_ROWS],
        member,
        (((1,), (0,)), ((), ())),
        precision=lax.Precision.HIGHEST,
        preferred_element_type=jnp.float32,
    )
    join = HALF_ROWS - PLANE
    for field, target in ((0, signal), (1, back)):
        upper = jnp.where(odd_slab, upper_chip[field], upper_core[field]).astype(jnp.float32)
        target[0:join] = lower_grids[field, 0:join]
        target[join:HALF_ROWS] = lower_grids[field, join:HALF_ROWS] + upper[0:PLANE]
        target[HALF_ROWS:] = upper[PLANE:HALF_ROWS]
    estimate = jnp.sum(signal[...], axis=0, keepdims=True)
    for _ in range(ITERS):
        weight_var = back[...] + jnp.maximum(estimate, 0.0) * chosen[...] + 1.0
        ratio = chosen[...] / weight_var
        upper_sum = jnp.sum(ratio * signal[...], axis=0, keepdims=True)
        lower_sum = jnp.sum(ratio * chosen[...], axis=0, keepdims=True)
        estimate = upper_sum / lower_sum
    devices = estimates.shape[0]
    target = lax.broadcasted_iota(jnp.int32, (devices, LANES), 0) * 2
    for j in range(2):
        held = jnp.where(slots[...] == target + j, estimate, 0.0)
        estimates[:, j : j + 1] = jnp.sum(held, axis=1, keepdims=True)


def slot_numbers(owners):
    position = jnp.arange(owners.shape[0], dtype=jnp.int32)
    earlier = (owners[None, :] == owners[:, None]) & (position[None, :] < position[:, None])
    return owners * 2 + jnp.sum(jnp.where(earlier, 1, 0), axis=1).astype(jnp.int32)


def pairs_even(count):
    return [(i, i ^ 1) for i in range(count)]


def pairs_odd(count):
    return [(i, i + 1 if i % 2 else i - 1) for i in range(1, count - 1)]


def summed_over_devices(sums):
    half = sums.shape[0] // 2
    core = lax.axis_index("frame") % 2
    mine = lax.dynamic_slice_in_dim(sums, core * half, half, 0)
    other = lax.dynamic_slice_in_dim(sums, (1 - core) * half, half, 0)

    def swapped(x, axis, flip):
        return lax.ppermute(x, axis, [(i, i ^ flip) for i in range(lax.axis_size(axis))])

    held = mine + swapped(other, "frame", 1)
    for axis, flips in (("refl", (1, 2, 3)), ("refl", (4, 8, 12)), ("frame", (2, 4, 6))):
        arrived = [swapped(held, axis, flip) for flip in flips]
        held = held + (arrived[0] + (arrived[1] + arrived[2]))
    rest = swapped(held, "frame", 1)
    return jnp.where(
        core == 0, jnp.concatenate([held, rest], axis=0), jnp.concatenate([rest, held], axis=0)
    )


def per_device(image, gain, pixel_mask, anchor_row, anchor_col, owner, region):
    frames, height, columns = image.shape
    slabs = lax.axis_size("frame")
    bands = lax.axis_size("refl")
    slab = lax.axis_index("frame")
    band = lax.axis_index("refl")
    place = jnp.stack([band % 2, slab % 2, jnp.where(slab > 0, 1, 0)]).astype(jnp.int32)
    f32 = jnp.float32
    smem = pl.BlockSpec(memory_space=pltpu.SMEM)
    vmem = pl.BlockSpec(memory_space=pltpu.VMEM)

    edge_shape = jax.ShapeDtypeStruct((HALO + 1, frames, columns), f32)
    first, second = pl.pallas_call(
        edge_kernel,
        grid=(1,),
        in_specs=[
            smem,
            pl.BlockSpec((frames, 8, columns), lambda i: (0, 0, 0)),
            pl.BlockSpec((frames, 8, columns), lambda i: (0, height // 8 - 1, 0)),
            pl.BlockSpec((height, columns), lambda i: (0, 0)),
            pl.BlockSpec((height, columns), lambda i: (0, 0)),
        ],
        out_specs=[pl.BlockSpec((HALO + 1, frames, columns), lambda i: (0, 0, 0))] * 2,
        out_shape=[edge_shape, edge_shape],
        name="edges",
    )(place, image, image, gain, pixel_mask)
    halo_first = lax.ppermute(first, "refl", pairs_even(bands))
    halo_second = lax.ppermute(second, "refl", pairs_odd(bands))

    own = jnp.stack([anchor_row, anchor_col, region[:, 0]])
    from_core = lax.ppermute(own, "frame", pairs_even(slabs))
    from_chip = lax.ppermute(own, "frame", pairs_odd(slabs))
    slots = slot_numbers(owner[:, 0])[None, :]

    corrected, totals = pl.pallas_call(
        level_kernel,
        in_specs=[smem] + [vmem] * 6,
        out_specs=[vmem] * 2,
        out_shape=[
            jax.ShapeDtypeStruct((height, frames, columns), f32),
            jax.ShapeDtypeStruct((2, LANES), f32),
        ],
        compiler_params=PARAMS,
        name="levels",
    )(place, image, gain, pixel_mask, own, from_core, from_chip)
    totals_core = lax.ppermute(totals, "frame", pairs_even(slabs))
    totals_chip = lax.ppermute(totals, "frame", pairs_odd(slabs))

    mixer = jnp.asarray(depth_mixer(height, frames), jnp.bfloat16)
    bf16 = jnp.bfloat16
    strong, lower_grids, upper_grids, partial = pl.pallas_call(
        spot_kernel,
        in_specs=[smem] + [vmem] * 11,
        out_specs=[vmem] * 4,
        out_shape=[
            jax.ShapeDtypeStruct((frames, height, columns), bf16),
            jax.ShapeDtypeStruct((2, HALF_ROWS, LANES), f32),
            jax.ShapeDtypeStruct((2, HALF_ROWS, LANES), f32),
            jax.ShapeDtypeStruct((REGIONS, WIDE_ROWS), f32),
        ],
        scratch_shapes=[
            pltpu.VMEM((height + 2 * HALO, frames, columns), f32),
            pltpu.VMEM((height + 16, columns), f32),
            pltpu.VMEM((3, height, columns), f32),
            pltpu.VMEM((height, frames, columns), f32),
            pltpu.VMEM((3, height * frames, columns), bf16),
            pltpu.VMEM((2, columns, GRID * LANES), bf16),
            pltpu.VMEM((height * 8, GRID * LANES), f32),
            pltpu.VMEM((PLANE * 8, LANES), f32),
            pltpu.VMEM((WIDE_ROWS, 2 * LANES), f32),
        ],
        compiler_params=PARAMS,
        name="spots",
    )(
        place,
        corrected,
        pixel_mask,
        halo_first,
        halo_second,
        own,
        from_core,
        from_chip,
        totals,
        totals_core,
        totals_chip,
        mixer,
    )
    upper_sent = upper_grids.astype(bf16)
    upper_core = lax.ppermute(upper_sent, "frame", pairs_even(slabs))
    upper_chip = lax.ppermute(upper_sent, "frame", pairs_odd(slabs))
    sums = summed_over_devices(partial)

    devices = slabs * bands
    profiles, estimates = pl.pallas_call(
        fit_kernel,
        in_specs=[smem] + [vmem] * 6,
        out_specs=[vmem] * 2,
        out_shape=[
            jax.ShapeDtypeStruct((REGIONS, GRID * GRID * GRID), f32),
            jax.ShapeDtypeStruct((devices, 2), f32),
        ],
        scratch_shapes=[pltpu.VMEM((FULL_ROWS, LANES), f32)] * 3,
        compiler_params=PARAMS,
        name="fit",
    )(place, sums, own, slots, lower_grids, upper_core, upper_chip)
    arrived = lax.all_to_all(estimates, ("frame", "refl"), split_axis=0, concat_axis=0, tiled=True)
    return (strong, arrived.reshape(1, devices * 2), profiles)


def solution(mesh):
    in_specs = (
        P("frame", "refl", None),
        P("refl", None),
        P("refl", None),
        P(("frame", "refl")),
        P(("frame", "refl")),
        P(("frame", "refl"), None),
        P(("frame", "refl"), None),
    )
    out_specs = (P("frame", "refl", None), P(("frame", "refl"), None), P())
    return jax.shard_map(
        per_device, mesh=mesh, in_specs=in_specs, out_specs=out_specs, check_vma=False
    )
```

```python
import functools

import jax
import jax.numpy as jnp
import numpy as np
from jax import lax
from jax.experimental import pallas as pl
from jax.experimental.pallas import tpu as pltpu
from jax.sharding import PartitionSpec as P

SB_EDGE = 16
GRID = 9
REGIONS = 32
ITERS = 3
HALO = 3
LANES = 128
HALF_BINS = 5
PLANE = 88
HALF_ROWS = HALF_BINS * PLANE
FULL_ROWS = GRID * PLANE
WIDE_ROWS = 896
PARAMS = pltpu.CompilerParams(vmem_limit_bytes=48 * 1024 * 1024)


def tent_values():
    centres = (np.arange(SB_EDGE, dtype=np.float32) + 0.5) * (GRID / SB_EDGE)
    bins = np.arange(GRID, dtype=np.float32) + 0.5
    return np.maximum(0.0, 1.0 - np.abs(centres[None, :] - bins[:, None]))


TENT = tent_values()
EDGE_WEIGHT = TENT.sum(axis=0)


def depth_mixer(rows, frames):
    mixer = np.zeros((2, rows, 8, rows, frames), np.float32)
    for row in range(rows):
        mixer[0, row, :HALF_BINS, row, :] = TENT[:HALF_BINS, :frames]
        mixer[1, row, :HALF_BINS, row, :] = TENT[GRID - HALF_BINS :, frames:]
    return mixer.reshape(2, rows * 8, rows * frames)


def dot(a, b):
    return lax.dot_general(a, b, (((1,), (0,)), ((), ())), preferred_element_type=jnp.float32)


def dot_nt(a, b):
    return lax.dot_general(a, b, (((1,), (1,)), ((), ())), preferred_element_type=jnp.float32)


def split_two(x):
    high = x.astype(jnp.bfloat16)
    return high, (x - high.astype(jnp.float32)).astype(jnp.bfloat16)


def parity(axis):
    return lax.axis_index(axis) % 2 == 1


def send_kernel(
    image,
    gain,
    mask,
    row,
    column,
    region,
    first,
    second,
    core,
    chip,
    kept,
    counts_in,
    gains,
    masks,
    infos,
    arrived,
):
    frames, height, columns = image.shape
    odd_band = parity("refl")
    odd_slab = parity("frame")
    copies = [(image, counts_in), (gain, gains), (mask, masks)]
    copies += [(info, infos.at[k]) for k, info in enumerate((row, column, region))]
    copies = [pltpu.make_async_copy(*copy, arrived.at[k]) for k, copy in enumerate(copies)]
    for copy in copies:
        copy.start()
    for copy in copies:
        copy.wait()
    live = masks[...].astype(jnp.float32)
    values = counts_in[...] * (gains[...] * live)[None]
    kept[0:height] = jnp.transpose(values, (1, 0, 2))

    head, tail = kept[0:HALO], kept[height - HALO : height]
    first[0:HALO] = jnp.where(odd_band, head, tail)
    second[0:HALO] = jnp.where(odd_band, tail, head)
    head, tail = live[0:HALO], live[height - HALO :]
    first[HALO, 0:HALO] = jnp.where(odd_band, head, tail)
    second[HALO, 0:HALO] = jnp.where(odd_band, tail, head)

    counts = values.astype(jnp.bfloat16).astype(jnp.float32)
    inner = counts[1]
    for z in range(2, frames - 1):
        inner = inner + counts[z]
    border = float(EDGE_WEIGHT[0])
    lower = inner + counts[frames - 1] + border * counts[0]
    upper = inner + counts[0] + border * counts[frames - 1]
    core[0:height] = jnp.where(odd_slab, upper, lower)
    chip[0:height] = jnp.where(odd_slab, lower, upper)
    for k in range(3):
        sent = infos[k].astype(jnp.float32)
        core[height + k : height + k + 1, 0:LANES] = sent
        chip[height + k : height + k + 1, 0:LANES] = sent
        kept[height, k : k + 1, 0:LANES] = sent
    for place, whole in enumerate((live, lower, upper)):
        first_row = height + 1 + place * height // 8
        kept[first_row : first_row + height // 8] = whole.reshape(height // 8, 8, columns)


def kept_info(kept, height, k):
    return kept[height, k : k + 1, 0:LANES].astype(jnp.int32)


def kept_rows(kept, height, place):
    first_row = height + 1 + place * height // 8
    return kept[first_row : first_row + height // 8].reshape(height, kept.shape[2])


def shoebox_offsets(anchors, extent):
    return lax.broadcasted_iota(jnp.int32, (extent, LANES), 0) - anchors


def total_weights(anchors, extent):
    offset = shoebox_offsets(anchors, extent)
    inside = (offset >= 0) & (offset < SB_EDGE)
    border = (offset == 0) | (offset == SB_EDGE - 1)
    return jnp.where(border, float(EDGE_WEIGHT[0]), jnp.where(inside, 1.0, 0.0))


def count_totals(levels, row, column):
    height, columns = levels.shape
    high, low = split_two(levels)
    by_column = total_weights(column, columns).astype(jnp.bfloat16)
    sums = dot(high, by_column) + dot(low, by_column)
    return jnp.sum(sums * total_weights(row, height), axis=0, keepdims=True)


def column_tents(column, columns, tents):
    offset = shoebox_offsets(column, columns)
    centre = (offset.astype(jnp.float32) + 0.5) * (GRID / SB_EDGE)
    for c in range(GRID):
        tent = jnp.maximum(1.0 - jnp.abs(centre - (c + 0.5)), 0.0)
        if c == 0:
            tent = jnp.where(offset >= 0, tent, 0.0)
        if c == GRID - 1:
            tent = jnp.where(offset < SB_EDGE, tent, 0.0)
        tents[:, c * LANES : (c + 1) * LANES] = tent.astype(jnp.bfloat16)


def window_sums(x):
    width = x.shape[-1]
    axis = x.ndim - 1
    pairs = x + pltpu.roll(x, 1, axis)
    fours = pairs + pltpu.roll(pairs, 2, axis)
    return fours + pltpu.roll(fours, width - 3, axis) - x


def window_counts(mask_rows, start, rows, terms, at):
    count = mask_rows[start : start + rows, :]
    for k in range(1, 2 * HALO + 1):
        count = count + mask_rows[start + k : start + k + rows, :]
    columns = count.shape[-1]
    tail = jnp.zeros((rows, LANES), jnp.float32)
    count = window_sums(jnp.concatenate([count, tail], axis=1))[:, 0:columns]
    per_spread = 1.0 / jnp.maximum(count - 1.0, 1.0)
    terms[0, at : at + rows, :] = 1.0 / jnp.maximum(count, 1.0)
    terms[1, at : at + rows, :] = per_spread
    terms[2, at : at + rows, :] = 1.0 + 6.0 * jnp.sqrt(2.0 * per_spread)


def row_pair(padded, base, terms, term_row, mask_rows, live_row, strong_rows, fields, slot):
    frames, columns = padded.shape[1:]
    rows = [padded[base + k] for k in range(2 * HALO + 2)]
    shared = rows[1]
    for k in range(2, 2 * HALO + 1):
        shared = shared + rows[k]
    squares = [x * x for x in rows]
    shared_square = squares[1]
    for k in range(2, 2 * HALO + 1):
        shared_square = shared_square + squares[k]
    frame_tail = jnp.zeros((2, frames, LANES), jnp.float32)
    total = jnp.stack([shared + rows[0], shared + rows[-1]])
    square = jnp.stack([shared_square + squares[0], shared_square + squares[-1]])
    total = window_sums(jnp.concatenate([total, frame_tail], axis=2))[:, :, 0:columns]
    square = window_sums(jnp.concatenate([square, frame_tail], axis=2))[:, :, 0:columns]
    value = jnp.stack([rows[HALO], rows[HALO + 1]])

    def every_frame(row):
        return jnp.broadcast_to(row, (frames, columns))

    def term(j):
        return jnp.stack([every_frame(terms[j, pl.ds(term_row + k, 1), :]) for k in range(2)])

    live = jnp.stack([every_frame(mask_rows[pl.ds(live_row + k, 1), :]) for k in range(2)])
    background = total * term(0)
    variance = (square - total * background) * term(1)
    per_root = lax.rsqrt(background + 1.0)
    excess = 2.0 * (variance * (per_root * per_root) - term(2))
    peak = (value - background - 3.0 * jnp.sqrt(background)) * per_root
    weight = live / ((1.0 + jnp.exp(-excess)) * (1.0 + jnp.exp(-peak)))
    weight_b = weight.astype(jnp.bfloat16).astype(jnp.float32)
    value_b = value.astype(jnp.bfloat16).astype(jnp.float32)
    background_b = background.astype(jnp.bfloat16).astype(jnp.float32)
    strong_rows[pl.ds(2 * slot, 2)] = weight_b
    at = pl.ds(pl.multiple_of(slot * 2 * frames, 2 * frames), 2 * frames)
    flat = (2 * frames, columns)
    fields[0, at, :] = (value_b - background_b).reshape(flat).astype(jnp.bfloat16)
    fields[1, at, :] = background_b.reshape(flat).astype(jnp.bfloat16)
    fields[2, at, :] = (weight_b * value_b).reshape(flat).astype(jnp.bfloat16)


def inner_kernel(kept, strong_rows, fields, tents, live, terms):
    height, columns = live.shape
    live[...] = kept_rows(kept, height, 0)
    column_tents(kept_info(kept, height, 1), columns, tents)
    rows = height - 8
    window_counts(live, 1, rows, terms, 0)

    def pair(i, carry):
        row_pair(kept, 2 * i + 1, terms, 2 * i, live, 2 * i + 4, strong_rows, fields, i)
        return carry

    lax.fori_loop(0, rows // 2, pair, 0, unroll=2)


def half_grids(mixed, tents, anchors, spread, packed, take):
    height = mixed.shape[0] // 8
    shift = jnp.broadcast_to(anchors, (8, LANES))
    spread[...] = dot(mixed, tents[...])
    bits = [(shift & (1 << k)) != 0 for k in range(5)]

    def one_column(c, carry):
        at = pl.ds(pl.multiple_of(c * LANES, LANES), LANES)
        rows = [spread[8 * r : 8 * r + 8, at] for r in range(height)]
        rows = [
            jnp.where(bits[4], rows[r + 16], rows[r]) if r + 16 < height else rows[r]
            for r in range(31)
        ]
        for k in (3, 2, 1, 0):
            keep = 16 + (1 << k) - 1
            rows = [jnp.where(bits[k], rows[r + (1 << k)], rows[r]) for r in range(keep)]
        for b in range(GRID):
            value = None
            for y in range(SB_EDGE):
                if TENT[b, y] != 0.0:
                    term = rows[y] * float(TENT[b, y])
                    value = term if value is None else value + term
            packed[pl.ds(pl.multiple_of((b * GRID + c) * 8, 8), 8), :] = value
        return carry

    lax.fori_loop(0, GRID, one_column, 0)
    for a in range(HALF_BINS):
        take(a, packed[pl.ds(a, PLANE, stride=8), :])


def clear_tail(packed):
    used = GRID * GRID * 8
    packed[used:, :] = jnp.zeros((packed.shape[0] - used, LANES), jnp.float32)


def spot_kernel(
    kept,
    halo_first,
    halo_second,
    from_core,
    from_chip,
    mixer,
    inner_fields,
    own_tents,
    edge_strong,
    edge_fields,
    partner_tents,
    rows,
    partial,
    padded,
    mask_rows,
    terms,
    field,
    spread,
    packed,
    contributions,
):
    frames, columns = kept.shape[1:]
    height = field.shape[0] // frames
    odd_band = parity("refl")
    odd_slab = parity("frame")
    has_partner = lax.axis_index("frame") > 0

    halo_a = halo_first[...]
    halo_b = halo_second[...]
    before = jnp.where(odd_band, halo_a, halo_b)
    after = jnp.where(odd_band, halo_b, halo_a)
    near = 4 + HALO
    padded[0:HALO] = before[0:HALO]
    padded[HALO : HALO + near] = kept[0:near]
    padded[HALO + near : HALO + 2 * near] = kept[height - near : height]
    padded[HALO + 2 * near :] = after[0:HALO]
    live = kept_rows(kept, height, 0)
    mask_rows[8 - HALO : 8, :] = before[HALO, 0:HALO]
    mask_rows[8 : 8 + near, :] = live[0:near]
    mask_rows[24 - HALO : 24 - HALO + near, :] = live[height - near :]
    mask_rows[28:31, :] = after[HALO, 0:HALO]
    window_counts(mask_rows, 5, 4, terms, 0)
    window_counts(mask_rows, 21, 4, terms, 8)
    for slot, (base, term_row, live_row) in enumerate(((0, 0, 8), (2, 2, 10), (10, 8, 24), (12, 10, 26))):
        row_pair(padded, base, terms, term_row, mask_rows, live_row, edge_strong, edge_fields, slot)

    partner = jnp.where(odd_slab, from_core[...], from_chip[...])
    following = jnp.where(odd_slab, from_chip[0:height], from_core[0:height])
    lower = kept_rows(kept, height, 1)
    upper = kept_rows(kept, height, 2)
    infos = [kept_info(kept, height, k) for k in range(3)]
    partner_info = [partner[height + k : height + k + 1, 0:LANES].astype(jnp.int32) for k in range(3)]
    rows[0] = infos[0]
    rows[1] = partner_info[0]
    own_total = count_totals(lower + following, infos[0], infos[1])
    partner_total = count_totals(partner[0:height] + upper, partner_info[0], partner_info[1])
    partner_total = jnp.where(has_partner, partner_total, 1.0)
    column_tents(partner_info[1], columns, partner_tents)

    contributions[...] = jnp.zeros(contributions.shape, jnp.float32)
    clear_tail(packed)
    quarter = 4 * frames
    field[0:quarter] = edge_fields[2, 0:quarter]
    field[quarter : height * frames - quarter] = inner_fields[2]
    field[height * frames - quarter :] = edge_fields[2, quarter:]
    for half, (anchors, tents, total) in enumerate(
        ((infos[0], own_tents, own_total), (partner_info[0], partner_tents, partner_total))
    ):
        mixed = dot(mixer[half], field[...]).astype(jnp.bfloat16)
        per_total = 1.0 / total

        def take(a, plane):
            first = (a + half * (GRID - HALF_BINS)) * PLANE
            contributions[first : first + PLANE, half * LANES : (half + 1) * LANES] = plane * per_total

        half_grids(mixed, tents, anchors, spread, packed, take)

    regions = lax.broadcasted_iota(jnp.int32, (REGIONS, LANES), 0)
    own_member = jnp.where(regions == infos[2], 1.0, 0.0)
    partner_member = jnp.where((regions == partner_info[2]) & has_partner, 1.0, 0.0)
    members = jnp.concatenate([own_member, partner_member], axis=1).astype(jnp.bfloat16)
    high, low = split_two(contributions[...])
    partial[...] = dot_nt(members, high) + dot_nt(members, low)


def grid_kernel(half, rows, mixer, edge_fields, inner_fields, tents, grids, field, spread, packed):
    clear_tail(packed)
    total = field.shape[0]
    quarter = edge_fields.shape[1] // 2
    for k in range(2):
        field[0:quarter] = edge_fields[k, 0:quarter]
        field[quarter : total - quarter] = inner_fields[k]
        field[total - quarter :] = edge_fields[k, quarter:]
        mixed = dot(mixer[half], field[...]).astype(jnp.bfloat16)

        def take(a, plane):
            grids[k, a * PLANE : (a + 1) * PLANE, :] = plane.astype(grids.dtype)

        half_grids(mixed, tents, rows[half], spread, packed, take)


def strong_kernel(edge_strong, inner_strong, strong, rows):
    rows[0:4] = edge_strong[0:4]
    rows[4 : rows.shape[0] - 4] = inner_strong[...]
    rows[rows.shape[0] - 4 :] = edge_strong[4:]
    strong[...] = jnp.transpose(rows[...], (1, 0, 2)).astype(jnp.bfloat16)


def fit_kernel(sums, region, slots, lower_grids, upper_core, upper_chip, estimates, signal, back, chosen):
    odd_slab = parity("frame")
    total = jnp.sum(sums[...], axis=1, keepdims=True)
    profile = sums[...] / total
    regions = lax.broadcasted_iota(jnp.int32, (REGIONS, LANES), 0)
    member = jnp.where(regions == region[...], 1.0, 0.0)
    chosen[...] = lax.dot_general(
        jnp.transpose(profile, (1, 0))[0:FULL_ROWS],
        member,
        (((1,), (0,)), ((), ())),
        precision=lax.Precision.HIGHEST,
        preferred_element_type=jnp.float32,
    )
    join = HALF_ROWS - PLANE
    for field, target in ((0, signal), (1, back)):
        upper = jnp.where(odd_slab, upper_chip[field], upper_core[field]).astype(jnp.float32)
        target[0:join] = lower_grids[field, 0:join]
        target[join:HALF_ROWS] = lower_grids[field, join:HALF_ROWS] + upper[0:PLANE]
        target[HALF_ROWS:] = upper[PLANE:HALF_ROWS]
    estimate = jnp.sum(signal[...], axis=0, keepdims=True)
    for _ in range(ITERS):
        weight_var = back[...] + jnp.maximum(estimate, 0.0) * chosen[...] + 1.0
        ratio = chosen[...] / weight_var
        upper_sum = jnp.sum(ratio * signal[...], axis=0, keepdims=True)
        lower_sum = jnp.sum(ratio * chosen[...], axis=0, keepdims=True)
        estimate = upper_sum / lower_sum
    devices = estimates.shape[0]
    target = lax.broadcasted_iota(jnp.int32, (devices, LANES), 0) * 2
    for j in range(2):
        held = jnp.where(slots[...] == target + j, estimate, 0.0)
        estimates[:, j : j + 1] = jnp.sum(held, axis=1, keepdims=True)


def profile_kernel(sums, profiles):
    profile = sums[...] / jnp.sum(sums[...], axis=1, keepdims=True)
    profiles[...] = jnp.concatenate(
        [profile[:, a * PLANE : a * PLANE + GRID * GRID] for a in range(GRID)], axis=1
    )


def spread_kernel(arrived, intensity):
    devices = arrived.shape[0]
    lane = lax.broadcasted_iota(jnp.int32, (devices, 2 * devices), 1)
    source = lax.broadcasted_iota(jnp.int32, (devices, 2 * devices), 0)
    placed = jnp.where(lane == 2 * source, arrived[:, 0:1], 0.0)
    placed = placed + jnp.where(lane == 2 * source + 1, arrived[:, 1:2], 0.0)
    intensity[...] = jnp.sum(placed, axis=0, keepdims=True)


def slot_numbers(owners):
    position = jnp.arange(owners.shape[0], dtype=jnp.int32)
    earlier = (owners[None, :] == owners[:, None]) & (position[None, :] < position[:, None])
    return owners * 2 + jnp.sum(jnp.where(earlier, 1, 0), axis=1).astype(jnp.int32)


def pairs_even(count):
    return [(i, i ^ 1) for i in range(count)]


def pairs_odd(count):
    return [(i, i + 1 if i % 2 else i - 1) for i in range(1, count - 1)]


def swapped(x, axis, flip):
    return lax.ppermute(x, axis, [(i, i ^ flip) for i in range(lax.axis_size(axis))])


def summed_over_four(sums, axis, flips):
    sent = sums.astype(jnp.bfloat16)
    one, two, three = [swapped(sent, axis, flip).astype(jnp.float32) for flip in flips]
    return (sent.astype(jnp.float32) + one) + (two + three)


def per_device(image, gain, pixel_mask, anchor_row, anchor_col, owner, region):
    frames, height, columns = image.shape
    slabs = lax.axis_size("frame")
    bands = lax.axis_size("refl")
    devices = slabs * bands
    f32, bf16 = jnp.float32, jnp.bfloat16
    vmem = pl.BlockSpec(memory_space=pltpu.VMEM)

    def shape(dims, dtype=f32):
        return jax.ShapeDtypeStruct(dims, dtype)

    def call(kernel, operands, outs, scratch=(), name=None, work=1):
        return pl.pallas_call(
            kernel,
            in_specs=[vmem] * len(operands),
            out_specs=[vmem] * len(outs),
            out_shape=outs,
            scratch_shapes=[pltpu.VMEM(s.shape, s.dtype) for s in scratch],
            compiler_params=PARAMS,
            cost_estimate=pl.CostEstimate(flops=work, bytes_accessed=work, transcendentals=0),
            name=name,
        )(*operands)

    row, column, area = (x.reshape(1, -1) for x in (anchor_row, anchor_col, region))
    first, second, core, chip, kept = pl.pallas_call(
        send_kernel,
        in_specs=[pl.BlockSpec(memory_space=pl.ANY)] * 6,
        out_specs=[vmem] * 5,
        out_shape=[shape((HALO + 1, frames, columns))] * 2
        + [shape((height + 8, columns))] * 2
        + [shape((height + 1 + 3 * height // 8, frames, columns))],
        scratch_shapes=[
            pltpu.VMEM((frames, height, columns), f32),
            pltpu.VMEM((height, columns), f32),
            pltpu.VMEM((height, columns), jnp.int32),
            pltpu.VMEM((3, 1, LANES), jnp.int32),
            pltpu.SemaphoreType.DMA((6,)),
        ],
        name="sent",
    )(image, gain, pixel_mask, row, column, area)
    halo_second = lax.ppermute(second, "refl", pairs_odd(bands))
    halo_first = lax.ppermute(first, "refl", pairs_even(bands))
    from_core = lax.ppermute(core, "frame", pairs_even(slabs))
    from_chip = lax.ppermute(chip, "frame", pairs_odd(slabs))
    slots = slot_numbers(owner[:, 0])[None, :]

    inner = height - 8
    tent_shape = shape((columns, GRID * LANES), bf16)
    inner_strong, inner_fields, own_tents = call(
        inner_kernel,
        (kept,),
        [shape((inner, frames, columns)), shape((3, inner * frames, columns), bf16), tent_shape],
        [shape((height, columns)), shape((3, inner, columns))],
        name="inner",
    )

    mixer = jnp.asarray(depth_mixer(height, frames), bf16)
    field_shape = shape((height * frames, columns), bf16)
    spread_shape = shape((height * 8, GRID * LANES))
    packed_shape = shape((PLANE * 8, LANES))
    edge_strong, edge_fields, partner_tents, rows, partial = call(
        spot_kernel,
        (
            kept,
            halo_first,
            halo_second,
            from_core,
            from_chip,
            mixer,
            inner_fields,
            own_tents,
        ),
        [
            shape((8, frames, columns)),
            shape((3, 8 * frames, columns), bf16),
            tent_shape,
            shape((2, 1, LANES), jnp.int32),
            shape((REGIONS, WIDE_ROWS)),
        ],
        [
            shape((2 * (HALO + 4 + HALO), frames, columns)),
            shape((height, columns)),
            shape((3, 16, columns)),
            field_shape,
            spread_shape,
            packed_shape,
            shape((WIDE_ROWS, 2 * LANES)),
        ],
        name="spots",
    )
    sums = partial + swapped(partial, "frame", 1)
    sums, edge_fields = lax.optimization_barrier((sums, edge_fields))
    scratch = [field_shape, spread_shape, packed_shape]
    (upper_grids,) = call(
        functools.partial(grid_kernel, 1),
        (rows, mixer, edge_fields, inner_fields, partner_tents),
        [shape((2, HALF_ROWS, LANES), bf16)],
        scratch,
        name="upper",
    )
    sums = summed_over_four(sums, "refl", (1, 2, 3))
    sums, upper_grids, edge_fields = lax.optimization_barrier((sums, upper_grids, edge_fields))
    upper_core = lax.ppermute(upper_grids, "frame", pairs_even(slabs))
    upper_chip = lax.ppermute(upper_grids, "frame", pairs_odd(slabs))
    sums = summed_over_four(sums, "refl", (4, 8, 12))
    sums, edge_fields = lax.optimization_barrier((sums, edge_fields))
    (lower_grids,) = call(
        functools.partial(grid_kernel, 0),
        (rows, mixer, edge_fields, inner_fields, own_tents),
        [shape((2, HALF_ROWS, LANES))],
        scratch,
        name="lower",
    )
    sums = summed_over_four(sums, "frame", (2, 4, 6))
    (strong,) = call(
        strong_kernel,
        (edge_strong, inner_strong),
        [shape((frames, height, columns), bf16)],
        [shape((height, frames, columns))],
        name="strong",
    )
    (estimates,) = call(
        fit_kernel,
        (sums, area, slots, lower_grids, upper_core, upper_chip),
        [shape((devices, 2))],
        [shape((FULL_ROWS, LANES))] * 3,
        name="fit",
    )
    arrived = lax.all_to_all(estimates, ("frame", "refl"), split_axis=0, concat_axis=0, tiled=True)
    (profiles,) = call(profile_kernel, (sums,), [shape((REGIONS, GRID * GRID * GRID))], name="profiles")
    (intensity,) = call(spread_kernel, (arrived,), [shape((1, devices * 2))], name="intensity")
    return (strong, intensity, profiles)


def solution(mesh):
    in_specs = (
        P("frame", "refl", None),
        P("refl", None),
        P("refl", None),
        P(("frame", "refl")),
        P(("frame", "refl")),
        P(("frame", "refl"), None),
        P(("frame", "refl"), None),
    )
    out_specs = (P("frame", "refl", None), P(("frame", "refl"), None), P())
    return jax.shard_map(
        per_device, mesh=mesh, in_specs=in_specs, out_specs=out_specs, check_vma=False
    )
```

```python
import functools

import jax
import jax.numpy as jnp
import numpy as np
from jax import lax
from jax.experimental import pallas as pl
from jax.experimental.pallas import tpu as pltpu
from jax.sharding import PartitionSpec as P

SB_EDGE = 16
GRID = 9
REGIONS = 32
ITERS = 3
HALO = 3
LANES = 128
HALF_BINS = 5
PLANE = 88
HALF_ROWS = HALF_BINS * PLANE
FULL_ROWS = GRID * PLANE
WIDE_ROWS = 896
PARAMS = pltpu.CompilerParams(vmem_limit_bytes=24 * 1024 * 1024)


def tent_values():
    centres = (np.arange(SB_EDGE, dtype=np.float32) + 0.5) * (GRID / SB_EDGE)
    bins = np.arange(GRID, dtype=np.float32) + 0.5
    return np.maximum(0.0, 1.0 - np.abs(centres[None, :] - bins[:, None]))


TENT = tent_values()
EDGE_WEIGHT = TENT.sum(axis=0)


def depth_mixer(rows, frames):
    mixer = np.zeros((2, rows, 8, rows, frames), np.float32)
    for row in range(rows):
        mixer[0, row, :HALF_BINS, row, :] = TENT[:HALF_BINS, :frames]
        mixer[1, row, :HALF_BINS, row, :] = TENT[GRID - HALF_BINS :, frames:]
    return mixer.reshape(2, rows * 8, rows * frames)


def dot(a, b):
    return lax.dot_general(a, b, (((1,), (0,)), ((), ())), preferred_element_type=jnp.float32)


def dot_nt(a, b):
    return lax.dot_general(a, b, (((1,), (1,)), ((), ())), preferred_element_type=jnp.float32)


def split_two(x):
    high = x.astype(jnp.bfloat16)
    return high, (x - high.astype(jnp.float32)).astype(jnp.bfloat16)


def parity(axis):
    return lax.axis_index(axis) % 2 == 1


def send_kernel(
    image,
    gain,
    mask,
    row,
    column,
    region,
    first,
    second,
    core,
    chip,
    kept,
    counts_in,
    gains,
    masks,
    infos,
    arrived,
):
    frames, height, columns = image.shape
    odd_band = parity("refl")
    odd_slab = parity("frame")
    copies = [(image, counts_in), (gain, gains), (mask, masks)]
    copies += [(info, infos.at[k]) for k, info in enumerate((row, column, region))]
    copies = [pltpu.make_async_copy(*copy, arrived.at[k]) for k, copy in enumerate(copies)]
    for copy in copies:
        copy.start()
    for copy in copies:
        copy.wait()
    live = masks[...].astype(jnp.float32)
    values = counts_in[...] * (gains[...] * live)[None]
    kept[0:height] = jnp.transpose(values, (1, 0, 2))

    head, tail = kept[0:HALO], kept[height - HALO : height]
    first[0:HALO] = jnp.where(odd_band, head, tail)
    second[0:HALO] = jnp.where(odd_band, tail, head)
    head, tail = live[0:HALO], live[height - HALO :]
    first[HALO, 0:HALO] = jnp.where(odd_band, head, tail)
    second[HALO, 0:HALO] = jnp.where(odd_band, tail, head)

    counts = values.astype(jnp.bfloat16).astype(jnp.float32)
    inner = counts[1]
    for z in range(2, frames - 1):
        inner = inner + counts[z]
    border = float(EDGE_WEIGHT[0])
    lower = inner + counts[frames - 1] + border * counts[0]
    upper = inner + counts[0] + border * counts[frames - 1]
    core[0:height] = jnp.where(odd_slab, upper, lower)
    chip[0:height] = jnp.where(odd_slab, lower, upper)
    for k in range(3):
        sent = infos[k].astype(jnp.float32)
        core[height + k : height + k + 1, 0:LANES] = sent
        chip[height + k : height + k + 1, 0:LANES] = sent
        kept[height, k : k + 1, 0:LANES] = sent
    for place, whole in enumerate((live, lower, upper)):
        first_row = height + 1 + place * height // 8
        kept[first_row : first_row + height // 8] = whole.reshape(height // 8, 8, columns)


def kept_info(kept, height, k):
    return kept[height, k : k + 1, 0:LANES].astype(jnp.int32)


def kept_rows(kept, height, place):
    first_row = height + 1 + place * height // 8
    return kept[first_row : first_row + height // 8].reshape(height, kept.shape[2])


def shoebox_offsets(anchors, extent):
    return lax.broadcasted_iota(jnp.int32, (extent, LANES), 0) - anchors


def total_weights(anchors, extent):
    offset = shoebox_offsets(anchors, extent)
    inside = (offset >= 0) & (offset < SB_EDGE)
    border = (offset == 0) | (offset == SB_EDGE - 1)
    return jnp.where(border, float(EDGE_WEIGHT[0]), jnp.where(inside, 1.0, 0.0))


def count_totals(levels, row, column):
    height, columns = levels.shape
    high, low = split_two(levels)
    by_column = total_weights(column, columns).astype(jnp.bfloat16)
    sums = dot(high, by_column) + dot(low, by_column)
    return jnp.sum(sums * total_weights(row, height), axis=0, keepdims=True)


def column_tents(column, columns, tents):
    offset = shoebox_offsets(column, columns)
    offset = jnp.where(offset < 0, -2, jnp.where(offset >= SB_EDGE, SB_EDGE + 1, offset))
    centre = (offset.astype(jnp.float32) + 0.5) * (GRID / SB_EDGE) - GRID / 2
    centre = centre.astype(jnp.bfloat16)
    one, zero = jnp.bfloat16(1.0), jnp.bfloat16(0.0)
    for c in range(GRID):
        distance = jnp.abs(centre - jnp.bfloat16(c - GRID // 2))
        tents[:, c * LANES : (c + 1) * LANES] = jnp.maximum(one - distance, zero)


def window_sums(x):
    width = x.shape[-1]
    axis = x.ndim - 1
    pairs = x + pltpu.roll(x, 1, axis)
    fours = pairs + pltpu.roll(pairs, 2, axis)
    return fours + pltpu.roll(fours, width - 3, axis) - x


def window_counts(mask_rows, start, rows, terms, at):
    count = mask_rows[start : start + rows, :]
    for k in range(1, 2 * HALO + 1):
        count = count + mask_rows[start + k : start + k + rows, :]
    columns = count.shape[-1]
    tail = jnp.zeros((rows, LANES), jnp.float32)
    count = window_sums(jnp.concatenate([count, tail], axis=1))[:, 0:columns]
    per_spread = 1.0 / jnp.maximum(count - 1.0, 1.0)
    terms[0, at : at + rows, :] = 1.0 / jnp.maximum(count, 1.0)
    terms[1, at : at + rows, :] = 2.0 * per_spread
    terms[2, at : at + rows, :] = 2.0 + 12.0 * jnp.sqrt(2.0 * per_spread)


def row_pair(padded, base, terms, term_row, mask_rows, live_row, strong_rows, fields, slot):
    frames, columns = padded.shape[1:]
    rows = [padded[base + k] for k in range(2 * HALO + 2)]
    shared = rows[1]
    for k in range(2, 2 * HALO + 1):
        shared = shared + rows[k]
    squares = [x * x for x in rows]
    shared_square = squares[1]
    for k in range(2, 2 * HALO + 1):
        shared_square = shared_square + squares[k]
    frame_tail = jnp.zeros((2, frames, LANES), jnp.float32)
    total = jnp.stack([shared + rows[0], shared + rows[-1]])
    square = jnp.stack([shared_square + squares[0], shared_square + squares[-1]])
    total = window_sums(jnp.concatenate([total, frame_tail], axis=2))[:, :, 0:columns]
    square = window_sums(jnp.concatenate([square, frame_tail], axis=2))[:, :, 0:columns]
    value = jnp.stack([rows[HALO], rows[HALO + 1]])

    def every_frame(row):
        return jnp.broadcast_to(row, (frames, columns))

    def term(j):
        return jnp.stack([every_frame(terms[j, pl.ds(term_row + k, 1), :]) for k in range(2)])

    live = jnp.stack([every_frame(mask_rows[pl.ds(live_row + k, 1), :]) for k in range(2)])
    background = total * term(0)
    variance = (square - total * background) * term(1)
    per_root = lax.rsqrt(background + 1.0)
    root = background * lax.rsqrt(jnp.maximum(background, 1e-30))
    shortfall = term(2) - variance * (per_root * per_root)
    below = (background - value + 3.0 * root) * per_root
    gates = (1.0 + jnp.exp(shortfall)) * (1.0 + jnp.exp(below))
    weight = pl.reciprocal(gates, approx=True)
    weight = live * (weight * (2.0 - gates * weight))
    weight_b = weight.astype(jnp.bfloat16).astype(jnp.float32)
    value_b = value.astype(jnp.bfloat16).astype(jnp.float32)
    background_b = background.astype(jnp.bfloat16).astype(jnp.float32)
    strong_rows[pl.ds(2 * slot, 2)] = weight_b
    at = pl.ds(pl.multiple_of(slot * 2 * frames, 2 * frames), 2 * frames)
    flat = (2 * frames, columns)
    fields[0, at, :] = (value_b - background_b).reshape(flat).astype(jnp.bfloat16)
    fields[1, at, :] = background_b.reshape(flat).astype(jnp.bfloat16)
    fields[2, at, :] = (weight_b * value_b).reshape(flat).astype(jnp.bfloat16)


def inner_kernel(kept, strong_rows, fields, tents, live, terms):
    height, columns = live.shape
    live[...] = kept_rows(kept, height, 0)
    column_tents(kept_info(kept, height, 1), columns, tents)
    rows = height - 8
    window_counts(live, 1, rows, terms, 0)

    def pair(i, carry):
        row_pair(kept, 2 * i + 1, terms, 2 * i, live, 2 * i + 4, strong_rows, fields, i)
        return carry

    lax.fori_loop(0, rows // 2, pair, 0, unroll=6)


def half_grids(mixed, tents, anchors, spread, packed, take):
    height = mixed.shape[0] // 8
    shift = jnp.broadcast_to(anchors, (8, LANES))
    bits = [(shift & (1 << k)) != 0 for k in range(5)]

    def one_column(c, spread, at):
        rows = [spread[8 * r : 8 * r + 8, at] for r in range(height)]
        rows = [
            jnp.where(bits[4], rows[r + 16], rows[r]) if r + 16 < height else rows[r]
            for r in range(31)
        ]
        for k in (3, 2, 1, 0):
            keep = 16 + (1 << k) - 1
            rows = [jnp.where(bits[k], rows[r + (1 << k)], rows[r]) for r in range(keep)]
        for b in range(GRID):
            value = None
            for y in range(SB_EDGE):
                if TENT[b, y] != 0.0:
                    term = rows[y] * float(TENT[b, y])
                    value = term if value is None else value + term
            packed[(b * GRID + c) * 8 : (b * GRID + c) * 8 + 8, :] = value

    for c in range(0, GRID, 2):
        end = min(c + 2, GRID)
        slot = spread.at[c // 2 % 2]
        slot[:, 0 : (end - c) * LANES] = dot(mixed, tents[:, c * LANES : end * LANES])
        for k in range(end - c):
            one_column(c + k, slot, slice(k * LANES, (k + 1) * LANES))
    for a in range(HALF_BINS):
        take(a, packed[pl.ds(a, PLANE, stride=8), :])


def clear_tail(packed):
    used = GRID * GRID * 8
    packed[used:, :] = jnp.zeros((packed.shape[0] - used, LANES), jnp.float32)


def spot_kernel(
    kept,
    halo_first,
    halo_second,
    from_core,
    from_chip,
    mixer,
    inner_fields,
    own_tents,
    edge_strong,
    edge_fields,
    partner_tents,
    rows,
    kept_sums,
    sent_sums,
    padded,
    mask_rows,
    terms,
    field,
    spread,
    packed,
    contributions,
):
    frames, columns = kept.shape[1:]
    height = field.shape[0] // frames
    odd_band = parity("refl")
    odd_slab = parity("frame")
    has_partner = lax.axis_index("frame") > 0

    halo_a = halo_first[...]
    halo_b = halo_second[...]
    before = jnp.where(odd_band, halo_a, halo_b)
    after = jnp.where(odd_band, halo_b, halo_a)
    near = 4 + HALO
    padded[0:HALO] = before[0:HALO]
    padded[HALO : HALO + near] = kept[0:near]
    padded[HALO + near : HALO + 2 * near] = kept[height - near : height]
    padded[HALO + 2 * near :] = after[0:HALO]
    live = kept_rows(kept, height, 0)
    mask_rows[8 - HALO : 8, :] = before[HALO, 0:HALO]
    mask_rows[8 : 8 + near, :] = live[0:near]
    mask_rows[24 - HALO : 24 - HALO + near, :] = live[height - near :]
    mask_rows[28:31, :] = after[HALO, 0:HALO]
    window_counts(mask_rows, 5, 4, terms, 0)
    window_counts(mask_rows, 21, 4, terms, 8)
    for slot, (base, term_row, live_row) in enumerate(((0, 0, 8), (2, 2, 10), (10, 8, 24), (12, 10, 26))):
        row_pair(padded, base, terms, term_row, mask_rows, live_row, edge_strong, edge_fields, slot)

    partner = jnp.where(odd_slab, from_core[...], from_chip[...])
    following = jnp.where(odd_slab, from_chip[0:height], from_core[0:height])
    lower = kept_rows(kept, height, 1)
    upper = kept_rows(kept, height, 2)
    infos = [kept_info(kept, height, k) for k in range(3)]
    partner_info = [partner[height + k : height + k + 1, 0:LANES].astype(jnp.int32) for k in range(3)]
    rows[0] = infos[0]
    rows[1] = partner_info[0]
    own_total = count_totals(lower + following, infos[0], infos[1])
    partner_total = count_totals(partner[0:height] + upper, partner_info[0], partner_info[1])
    partner_total = jnp.where(has_partner, partner_total, 1.0)
    column_tents(partner_info[1], columns, partner_tents)

    contributions[...] = jnp.zeros(contributions.shape, jnp.float32)
    clear_tail(packed)
    quarter = 4 * frames
    field[0:quarter] = edge_fields[2, 0:quarter]
    field[quarter : height * frames - quarter] = inner_fields[2]
    field[height * frames - quarter :] = edge_fields[2, quarter:]
    for half, (anchors, tents, total) in enumerate(
        ((infos[0], own_tents, own_total), (partner_info[0], partner_tents, partner_total))
    ):
        mixed = dot(mixer[half], field[...]).astype(jnp.bfloat16)
        per_total = 1.0 / total

        def take(a, plane):
            first = (a + half * (GRID - HALF_BINS)) * PLANE
            contributions[first : first + PLANE, half * LANES : (half + 1) * LANES] = plane * per_total

        half_grids(mixed, tents, anchors, spread, packed, take)

    regions = lax.broadcasted_iota(jnp.int32, (REGIONS, LANES), 0)
    own_member = jnp.where(regions == infos[2], 1.0, 0.0)
    partner_member = jnp.where((regions == partner_info[2]) & has_partner, 1.0, 0.0)
    members = jnp.concatenate([own_member, partner_member], axis=1).astype(jnp.bfloat16)
    high, low = split_two(contributions[...])
    sums = dot_nt(members, high) + dot_nt(members, low)
    early, late = sums[0 : REGIONS // 2], sums[REGIONS // 2 :]
    kept_sums[...] = jnp.where(odd_slab, late, early)
    sent_sums[...] = jnp.where(odd_slab, early, late)


def grid_kernel(half, rows, mixer, edge_fields, inner_fields, tents, grids, field, spread, packed):
    clear_tail(packed)
    total = field.shape[0]
    quarter = edge_fields.shape[1] // 2
    for k in range(2):
        field[0:quarter] = edge_fields[k, 0:quarter]
        field[quarter : total - quarter] = inner_fields[k]
        field[total - quarter :] = edge_fields[k, quarter:]
        mixed = dot(mixer[half], field[...]).astype(jnp.bfloat16)

        def take(a, plane):
            grids[k, a * PLANE : (a + 1) * PLANE, :] = plane.astype(grids.dtype)

        half_grids(mixed, tents, rows[half], spread, packed, take)


def strong_kernel(edge_strong, inner_strong, strong, rows):
    rows[0:4] = edge_strong[0:4]
    rows[4 : rows.shape[0] - 4] = inner_strong[...]
    rows[rows.shape[0] - 4 :] = edge_strong[4:]
    strong[...] = jnp.transpose(rows[...], (1, 0, 2)).astype(jnp.bfloat16)


def all_regions(own_half, other_half):
    early = jnp.where(parity("frame"), other_half[...], own_half[...])
    late = jnp.where(parity("frame"), own_half[...], other_half[...])
    return jnp.concatenate([early, late], axis=0)


def fit_kernel(own_half, other_half, region, slots, lower_grids, upper_grids, estimates, signal, back, chosen):
    sums = all_regions(own_half, other_half)
    profile = sums / jnp.sum(sums, axis=1, keepdims=True)
    regions = lax.broadcasted_iota(jnp.int32, (REGIONS, LANES), 0)
    member = jnp.where(regions == region[...], 1.0, 0.0).astype(jnp.bfloat16)
    high, low = split_two(jnp.transpose(profile, (1, 0))[0:FULL_ROWS])
    chosen[...] = dot(high, member) + dot(low, member)
    join = HALF_ROWS - PLANE
    estimate = jnp.zeros((8, LANES), jnp.float32)
    for field, target in ((0, signal), (1, back)):
        upper = upper_grids[field].astype(jnp.float32)
        for r in range(0, FULL_ROWS, 8):
            value = lower_grids[field, r : r + 8] if r < HALF_ROWS else None
            if r >= join:
                late = upper[r - join : r - join + 8]
                value = late if value is None else value + late
            if field == 0:
                estimate = estimate + value
            target[r : r + 8] = value if field == 0 else value + 1.0
    estimate = jnp.sum(estimate, axis=0, keepdims=True)
    for _ in range(ITERS):
        level = jnp.broadcast_to(jnp.maximum(estimate, 0.0), (8, LANES))
        sums_up = [jnp.zeros((8, LANES), jnp.float32)] * 2
        sums_low = [jnp.zeros((8, LANES), jnp.float32)] * 2
        for r in range(0, FULL_ROWS, 8):
            share = chosen[r : r + 8]
            ratio = share / (back[r : r + 8] + level * share)
            k = r // 8 % 2
            sums_up[k] = sums_up[k] + ratio * signal[r : r + 8]
            sums_low[k] = sums_low[k] + ratio * share
        upper_sum = jnp.sum(sums_up[0] + sums_up[1], axis=0, keepdims=True)
        lower_sum = jnp.sum(sums_low[0] + sums_low[1], axis=0, keepdims=True)
        estimate = upper_sum / lower_sum
    devices = estimates.shape[0]
    target = lax.broadcasted_iota(jnp.int32, (devices, LANES), 0) * 2
    for j in range(2):
        held = jnp.where(slots[...] == target + j, estimate, 0.0)
        estimates[:, j : j + 1] = jnp.sum(held, axis=1, keepdims=True)


def profile_kernel(own_half, other_half, profiles):
    sums = all_regions(own_half, other_half)
    profile = sums / jnp.sum(sums, axis=1, keepdims=True)
    profiles[...] = jnp.concatenate(
        [profile[:, a * PLANE : a * PLANE + GRID * GRID] for a in range(GRID)], axis=1
    )


def spread_kernel(arrived, intensity):
    devices = arrived.shape[0]
    lane = lax.broadcasted_iota(jnp.int32, (devices, 2 * devices), 1)
    source = lax.broadcasted_iota(jnp.int32, (devices, 2 * devices), 0)
    placed = jnp.where(lane == 2 * source, arrived[:, 0:1], 0.0)
    placed = placed + jnp.where(lane == 2 * source + 1, arrived[:, 1:2], 0.0)
    intensity[...] = jnp.sum(placed, axis=0, keepdims=True)


def slot_numbers(owners):
    position = jnp.arange(owners.shape[0], dtype=jnp.int32)
    earlier = (owners[None, :] == owners[:, None]) & (position[None, :] < position[:, None])
    return owners * 2 + jnp.sum(jnp.where(earlier, 1, 0), axis=1).astype(jnp.int32)


def pairs_even(count):
    return [(i, i ^ 1) for i in range(count)]


def pairs_odd(count):
    return [(i, i + 1 if i % 2 else i - 1) for i in range(1, count - 1)]


def swapped(x, axis, flip):
    return lax.ppermute(x, axis, [(i, i ^ flip) for i in range(lax.axis_size(axis))])


def summed_over_four(sums, axis, flips):
    sent = sums.astype(jnp.bfloat16)
    one, two, three = [swapped(sent, axis, flip).astype(jnp.float32) for flip in flips]
    return (sent.astype(jnp.float32) + one) + (two + three)


def per_device(image, gain, pixel_mask, anchor_row, anchor_col, owner, region):
    frames, height, columns = image.shape
    slabs = lax.axis_size("frame")
    bands = lax.axis_size("refl")
    devices = slabs * bands
    f32, bf16 = jnp.float32, jnp.bfloat16
    vmem = pl.BlockSpec(memory_space=pltpu.VMEM)

    def shape(dims, dtype=f32):
        return jax.ShapeDtypeStruct(dims, dtype)

    def call(kernel, operands, outs, scratch=(), name=None, work=1):
        return pl.pallas_call(
            kernel,
            in_specs=[vmem] * len(operands),
            out_specs=[vmem] * len(outs),
            out_shape=outs,
            scratch_shapes=[pltpu.VMEM(s.shape, s.dtype) for s in scratch],
            compiler_params=PARAMS,
            cost_estimate=pl.CostEstimate(flops=work, bytes_accessed=work, transcendentals=0),
            name=name,
        )(*operands)

    row, column, area = (x.reshape(1, -1) for x in (anchor_row, anchor_col, region))
    first, second, core, chip, kept = pl.pallas_call(
        send_kernel,
        in_specs=[pl.BlockSpec(memory_space=pl.ANY)] * 6,
        out_specs=[vmem] * 5,
        out_shape=[shape((HALO + 1, frames, columns))] * 2
        + [shape((height + 8, columns))] * 2
        + [shape((height + 1 + 3 * height // 8, frames, columns))],
        scratch_shapes=[
            pltpu.VMEM((frames, height, columns), f32),
            pltpu.VMEM((height, columns), f32),
            pltpu.VMEM((height, columns), jnp.int32),
            pltpu.VMEM((3, 1, LANES), jnp.int32),
            pltpu.SemaphoreType.DMA((6,)),
        ],
        name="sent",
    )(image, gain, pixel_mask, row, column, area)
    halo_second = lax.ppermute(second, "refl", pairs_odd(bands))
    halo_first = lax.ppermute(first, "refl", pairs_even(bands))
    from_core = lax.ppermute(core, "frame", pairs_even(slabs))
    from_chip = lax.ppermute(chip, "frame", pairs_odd(slabs))
    slots = slot_numbers(owner[:, 0])[None, :]

    inner = height - 8
    tent_shape = shape((columns, GRID * LANES), bf16)
    inner_strong, inner_fields, own_tents = call(
        inner_kernel,
        (kept,),
        [shape((inner, frames, columns)), shape((3, inner * frames, columns), bf16), tent_shape],
        [shape((height, columns)), shape((3, inner, columns))],
        name="inner",
    )

    mixer = jnp.asarray(depth_mixer(height, frames), bf16)
    field_shape = shape((height * frames, columns), bf16)
    spread_shape = shape((2, height * 8, 2 * LANES))
    packed_shape = shape((PLANE * 8, LANES))
    edge_strong, edge_fields, partner_tents, rows, kept_sums, sent_sums = call(
        spot_kernel,
        (
            kept,
            halo_first,
            halo_second,
            from_core,
            from_chip,
            mixer,
            inner_fields,
            own_tents,
        ),
        [
            shape((8, frames, columns)),
            shape((3, 8 * frames, columns), bf16),
            tent_shape,
            shape((2, 1, LANES), jnp.int32),
            shape((REGIONS // 2, WIDE_ROWS)),
            shape((REGIONS // 2, WIDE_ROWS)),
        ],
        [
            shape((2 * (HALO + 4 + HALO), frames, columns)),
            shape((height, columns)),
            shape((3, 16, columns)),
            field_shape,
            spread_shape,
            packed_shape,
            shape((WIDE_ROWS, 2 * LANES)),
        ],
        name="spots",
    )
    sums = kept_sums + swapped(sent_sums, "frame", 1)
    sums, edge_fields = lax.optimization_barrier((sums, edge_fields))
    scratch = [field_shape, spread_shape, packed_shape]
    (upper_grids,) = call(
        functools.partial(grid_kernel, 1),
        (rows, mixer, edge_fields, inner_fields, partner_tents),
        [shape((2, HALF_ROWS, LANES), bf16)],
        scratch,
        name="upper",
    )
    sums = summed_over_four(sums, "refl", (1, 2, 3))
    sums, upper_grids, edge_fields = lax.optimization_barrier((sums, upper_grids, edge_fields))
    upper_grids = lax.ppermute(upper_grids, "frame", [(i + 1, i) for i in range(slabs - 1)])
    (lower_grids,) = call(
        functools.partial(grid_kernel, 0),
        (rows, mixer, edge_fields, inner_fields, own_tents),
        [shape((2, HALF_ROWS, LANES))],
        scratch,
        name="lower",
    )
    sums = summed_over_four(sums, "refl", (4, 8, 12))
    sums, lower_grids = lax.optimization_barrier((sums, lower_grids))
    sums = summed_over_four(sums, "frame", (2, 4, 6))
    other = swapped(sums, "frame", 1)
    (strong,) = call(
        strong_kernel,
        (edge_strong, inner_strong),
        [shape((frames, height, columns), bf16)],
        [shape((height, frames, columns))],
        name="strong",
    )
    (estimates,) = call(
        fit_kernel,
        (sums, other, area, slots, lower_grids, upper_grids),
        [shape((devices, 2))],
        [shape((FULL_ROWS, LANES))] * 3,
        name="fit",
    )
    arrived = lax.all_to_all(estimates, ("frame", "refl"), split_axis=0, concat_axis=0, tiled=True)
    (profiles,) = call(profile_kernel, (sums, other), [shape((REGIONS, GRID * GRID * GRID))], name="profiles")
    (intensity,) = call(spread_kernel, (arrived,), [shape((1, devices * 2))], name="intensity")
    return (strong, intensity, profiles)


def solution(mesh):
    in_specs = (
        P("frame", "refl", None),
        P("refl", None),
        P("refl", None),
        P(("frame", "refl")),
        P(("frame", "refl")),
        P(("frame", "refl"), None),
        P(("frame", "refl"), None),
    )
    out_specs = (P("frame", "refl", None), P(("frame", "refl"), None), P())
    return jax.shard_map(
        per_device, mesh=mesh, in_specs=in_specs, out_specs=out_specs, check_vma=False
    )
```

```python
import functools

import jax
import jax.numpy as jnp
import numpy as np
from jax import lax
from jax.experimental import pallas as pl
from jax.experimental.pallas import tpu as pltpu
from jax.sharding import PartitionSpec as P

SB_EDGE = 16
GRID = 9
REGIONS = 32
ITERS = 3
HALO = 3
LANES = 128
HALF_BINS = 5
PLANE = 88
HALF_ROWS = HALF_BINS * PLANE
FULL_ROWS = GRID * PLANE
WIDE_ROWS = 896
PARAMS = pltpu.CompilerParams(vmem_limit_bytes=24 * 1024 * 1024)


def tent_values():
    centres = (np.arange(SB_EDGE, dtype=np.float32) + 0.5) * (GRID / SB_EDGE)
    bins = np.arange(GRID, dtype=np.float32) + 0.5
    return np.maximum(0.0, 1.0 - np.abs(centres[None, :] - bins[:, None]))


TENT = tent_values()
EDGE_WEIGHT = TENT.sum(axis=0)


def depth_mixer(rows, frames):
    mixer = np.zeros((2, rows, 8, rows, frames), np.float32)
    for row in range(rows):
        mixer[0, row, :HALF_BINS, row, :] = TENT[:HALF_BINS, :frames]
        mixer[1, row, :HALF_BINS, row, :] = TENT[GRID - HALF_BINS :, frames:]
    return mixer.reshape(2, rows * 8, rows * frames)


def dot(a, b):
    return lax.dot_general(a, b, (((1,), (0,)), ((), ())), preferred_element_type=jnp.float32)


def dot_nt(a, b):
    return lax.dot_general(a, b, (((1,), (1,)), ((), ())), preferred_element_type=jnp.float32)


def split_two(x):
    high = x.astype(jnp.bfloat16)
    return high, (x - high.astype(jnp.float32)).astype(jnp.bfloat16)


def parity(axis):
    return lax.axis_index(axis) % 2 == 1


def send_kernel(
    image,
    gain,
    mask,
    row,
    column,
    region,
    first,
    second,
    core,
    chip,
    kept,
    counts_in,
    gains,
    masks,
    infos,
    arrived,
):
    frames, height, columns = image.shape
    odd_band = parity("refl")
    odd_slab = parity("frame")
    copies = [(image, counts_in), (gain, gains), (mask, masks)]
    copies += [(info, infos.at[k]) for k, info in enumerate((row, column, region))]
    copies = [pltpu.make_async_copy(*copy, arrived.at[k]) for k, copy in enumerate(copies)]
    for copy in copies:
        copy.start()
    for copy in copies:
        copy.wait()
    live = masks[...].astype(jnp.float32)
    values = counts_in[...] * (gains[...] * live)[None]
    kept[0:height] = jnp.transpose(values, (1, 0, 2))

    head, tail = kept[0:HALO], kept[height - HALO : height]
    first[0:HALO] = jnp.where(odd_band, head, tail)
    second[0:HALO] = jnp.where(odd_band, tail, head)
    head, tail = live[0:HALO], live[height - HALO :]
    first[HALO, 0:HALO] = jnp.where(odd_band, head, tail)
    second[HALO, 0:HALO] = jnp.where(odd_band, tail, head)

    counts = values.astype(jnp.bfloat16).astype(jnp.float32)
    inner = counts[1]
    for z in range(2, frames - 1):
        inner = inner + counts[z]
    border = float(EDGE_WEIGHT[0])
    lower = inner + counts[frames - 1] + border * counts[0]
    upper = inner + counts[0] + border * counts[frames - 1]
    core[0:height] = jnp.where(odd_slab, upper, lower)
    chip[0:height] = jnp.where(odd_slab, lower, upper)
    for k in range(3):
        sent = infos[k].astype(jnp.float32)
        core[height + k : height + k + 1, 0:LANES] = sent
        chip[height + k : height + k + 1, 0:LANES] = sent
        kept[height, k : k + 1, 0:LANES] = sent
    for place, whole in enumerate((live, lower, upper)):
        first_row = height + 1 + place * height // 8
        kept[first_row : first_row + height // 8] = whole.reshape(height // 8, 8, columns)


def kept_info(kept, height, k):
    return kept[height, k : k + 1, 0:LANES].astype(jnp.int32)


def kept_rows(kept, height, place):
    first_row = height + 1 + place * height // 8
    return kept[first_row : first_row + height // 8].reshape(height, kept.shape[2])


def shoebox_offsets(anchors, extent):
    return lax.broadcasted_iota(jnp.int32, (extent, LANES), 0) - anchors


def total_weights(anchors, extent):
    offset = shoebox_offsets(anchors, extent)
    inside = (offset >= 0) & (offset < SB_EDGE)
    border = (offset == 0) | (offset == SB_EDGE - 1)
    return jnp.where(border, float(EDGE_WEIGHT[0]), jnp.where(inside, 1.0, 0.0))


def count_totals(levels, row, column):
    height, columns = levels.shape
    high, low = split_two(levels)
    by_column = total_weights(column, columns).astype(jnp.bfloat16)
    sums = dot(high, by_column) + dot(low, by_column)
    return jnp.sum(sums * total_weights(row, height), axis=0, keepdims=True)


def column_tents(column, columns, tents):
    offset = shoebox_offsets(column, columns)
    offset = jnp.where(offset < 0, -2, jnp.where(offset >= SB_EDGE, SB_EDGE + 1, offset))
    centre = (offset.astype(jnp.float32) + 0.5) * (GRID / SB_EDGE) - GRID / 2
    centre = centre.astype(jnp.bfloat16)
    one, zero = jnp.bfloat16(1.0), jnp.bfloat16(0.0)
    for c in range(GRID):
        distance = jnp.abs(centre - jnp.bfloat16(c - GRID // 2))
        tents[:, c * LANES : (c + 1) * LANES] = jnp.maximum(one - distance, zero)


def window_sums(x):
    width = x.shape[-1]
    axis = x.ndim - 1
    pairs = x + pltpu.roll(x, 1, axis)
    fours = pairs + pltpu.roll(pairs, 2, axis)
    return fours + pltpu.roll(fours, width - 3, axis) - x


def window_counts(mask_rows, start, rows, terms, at):
    count = mask_rows[start : start + rows, :]
    for k in range(1, 2 * HALO + 1):
        count = count + mask_rows[start + k : start + k + rows, :]
    columns = count.shape[-1]
    tail = jnp.zeros((rows, LANES), jnp.float32)
    count = window_sums(jnp.concatenate([count, tail], axis=1))[:, 0:columns]
    per_spread = 1.0 / jnp.maximum(count - 1.0, 1.0)
    terms[0, at : at + rows, :] = 1.0 / jnp.maximum(count, 1.0)
    terms[1, at : at + rows, :] = 2.0 * per_spread
    terms[2, at : at + rows, :] = 2.0 + 12.0 * jnp.sqrt(2.0 * per_spread)


def row_pair(padded, base, terms, term_row, mask_rows, live_row, strong_rows, fields, slot):
    frames, columns = padded.shape[1:]
    rows = [padded[base + k] for k in range(2 * HALO + 2)]
    shared = rows[1]
    for k in range(2, 2 * HALO + 1):
        shared = shared + rows[k]
    squares = [x * x for x in rows]
    shared_square = squares[1]
    for k in range(2, 2 * HALO + 1):
        shared_square = shared_square + squares[k]
    frame_tail = jnp.zeros((2, frames, LANES), jnp.float32)
    total = jnp.stack([shared + rows[0], shared + rows[-1]])
    square = jnp.stack([shared_square + squares[0], shared_square + squares[-1]])
    total = window_sums(jnp.concatenate([total, frame_tail], axis=2))[:, :, 0:columns]
    square = window_sums(jnp.concatenate([square, frame_tail], axis=2))[:, :, 0:columns]
    value = jnp.stack([rows[HALO], rows[HALO + 1]])

    def every_frame(row):
        return jnp.broadcast_to(row, (frames, columns))

    def term(j):
        return jnp.stack([every_frame(terms[j, pl.ds(term_row + k, 1), :]) for k in range(2)])

    live = jnp.stack([every_frame(mask_rows[pl.ds(live_row + k, 1), :]) for k in range(2)])
    background = total * term(0)
    variance = (square - total * background) * term(1)
    per_root = lax.rsqrt(background + 1.0)
    root = background * lax.rsqrt(jnp.maximum(background, 1e-30))
    shortfall = term(2) - variance * (per_root * per_root)
    below = (background - value + 3.0 * root) * per_root
    gates = (1.0 + jnp.exp(shortfall)) * (1.0 + jnp.exp(below))
    weight = pl.reciprocal(gates, approx=True)
    weight = live * (weight * (2.0 - gates * weight))
    weight_b = weight.astype(jnp.bfloat16).astype(jnp.float32)
    value_b = value.astype(jnp.bfloat16).astype(jnp.float32)
    background_b = background.astype(jnp.bfloat16).astype(jnp.float32)
    strong_rows[pl.ds(2 * slot, 2)] = weight_b
    at = pl.ds(pl.multiple_of(slot * 2 * frames, 2 * frames), 2 * frames)
    flat = (2 * frames, columns)
    fields[0, at, :] = (value_b - background_b).reshape(flat).astype(jnp.bfloat16)
    fields[1, at, :] = background_b.reshape(flat).astype(jnp.bfloat16)
    fields[2, at, :] = (weight_b * value_b).reshape(flat).astype(jnp.bfloat16)


def inner_kernel(kept, strong_rows, fields, tents, live, terms):
    height, columns = live.shape
    live[...] = kept_rows(kept, height, 0)
    column_tents(kept_info(kept, height, 1), columns, tents)
    rows = height - 8
    window_counts(live, 1, rows, terms, 0)

    def pair(i, carry):
        row_pair(kept, 2 * i + 1, terms, 2 * i, live, 2 * i + 4, strong_rows, fields, i)
        return carry

    lax.fori_loop(0, rows // 2, pair, 0, unroll=6)


def half_grids(mixed, tents, anchors, spread, packed, take):
    height = mixed.shape[0] // 8
    shift = jnp.broadcast_to(anchors, (8, LANES))
    bits = [(shift & (1 << k)) != 0 for k in range(5)]

    def one_column(c, spread, at):
        rows = [spread[8 * r : 8 * r + 8, at] for r in range(height)]
        rows = [
            jnp.where(bits[4], rows[r + 16], rows[r]) if r + 16 < height else rows[r]
            for r in range(31)
        ]
        for k in (3, 2, 1, 0):
            keep = 16 + (1 << k) - 1
            rows = [jnp.where(bits[k], rows[r + (1 << k)], rows[r]) for r in range(keep)]
        for b in range(GRID):
            value = None
            for y in range(SB_EDGE):
                if TENT[b, y] != 0.0:
                    term = rows[y] * float(TENT[b, y])
                    value = term if value is None else value + term
            packed[(b * GRID + c) * 8 : (b * GRID + c) * 8 + 8, :] = value

    for c in range(0, GRID, 2):
        end = min(c + 2, GRID)
        slot = spread.at[c // 2 % 2]
        slot[:, 0 : (end - c) * LANES] = dot(mixed, tents[:, c * LANES : end * LANES])
        for k in range(end - c):
            one_column(c + k, slot, slice(k * LANES, (k + 1) * LANES))
    for a in range(HALF_BINS):
        take(a, packed[pl.ds(a, PLANE, stride=8), :])


def clear_tail(packed):
    used = GRID * GRID * 8
    packed[used:, :] = jnp.zeros((packed.shape[0] - used, LANES), jnp.float32)


def spot_kernel(
    kept,
    halo_first,
    halo_second,
    from_core,
    from_chip,
    mixer,
    inner_fields,
    own_tents,
    edge_strong,
    edge_fields,
    partner_tents,
    rows,
    kept_sums,
    sent_sums,
    padded,
    mask_rows,
    terms,
    field,
    spread,
    packed,
    contributions,
):
    frames, columns = kept.shape[1:]
    height = field.shape[0] // frames
    odd_band = parity("refl")
    odd_slab = parity("frame")
    has_partner = lax.axis_index("frame") > 0

    halo_a = halo_first[...]
    halo_b = halo_second[...]
    band = lax.axis_index("refl")
    before = jnp.where(odd_band, halo_a, jnp.where(band > 0, halo_b, 0.0))
    after = jnp.where(odd_band, jnp.where(band < lax.axis_size("refl") - 1, halo_b, 0.0), halo_a)
    near = 4 + HALO
    padded[0:HALO] = before[0:HALO]
    padded[HALO : HALO + near] = kept[0:near]
    padded[HALO + near : HALO + 2 * near] = kept[height - near : height]
    padded[HALO + 2 * near :] = after[0:HALO]
    live = kept_rows(kept, height, 0)
    mask_rows[8 - HALO : 8, :] = before[HALO, 0:HALO]
    mask_rows[8 : 8 + near, :] = live[0:near]
    mask_rows[24 - HALO : 24 - HALO + near, :] = live[height - near :]
    mask_rows[28:31, :] = after[HALO, 0:HALO]
    window_counts(mask_rows, 5, 4, terms, 0)
    window_counts(mask_rows, 21, 4, terms, 8)
    for slot, (base, term_row, live_row) in enumerate(((0, 0, 8), (2, 2, 10), (10, 8, 24), (12, 10, 26))):
        row_pair(padded, base, terms, term_row, mask_rows, live_row, edge_strong, edge_fields, slot)

    partner = jnp.where(odd_slab, from_core[...], from_chip[...])
    following = jnp.where(odd_slab, from_chip[0:height], from_core[0:height])
    following = jnp.where(lax.axis_index("frame") < lax.axis_size("frame") - 1, following, 0.0)
    lower = kept_rows(kept, height, 1)
    upper = kept_rows(kept, height, 2)
    infos = [kept_info(kept, height, k) for k in range(3)]
    partner_info = [partner[height + k : height + k + 1, 0:LANES].astype(jnp.int32) for k in range(3)]
    rows[0] = infos[0]
    rows[1] = partner_info[0]
    own_total = count_totals(lower + following, infos[0], infos[1])
    partner_total = count_totals(partner[0:height] + upper, partner_info[0], partner_info[1])
    partner_total = jnp.where(has_partner, partner_total, 1.0)
    column_tents(partner_info[1], columns, partner_tents)

    contributions[...] = jnp.zeros(contributions.shape, jnp.float32)
    clear_tail(packed)
    quarter = 4 * frames
    field[0:quarter] = edge_fields[2, 0:quarter]
    field[quarter : height * frames - quarter] = inner_fields[2]
    field[height * frames - quarter :] = edge_fields[2, quarter:]
    for half, (anchors, tents, total) in enumerate(
        ((infos[0], own_tents, own_total), (partner_info[0], partner_tents, partner_total))
    ):
        mixed = dot(mixer[half], field[...]).astype(jnp.bfloat16)
        per_total = 1.0 / total

        def take(a, plane):
            first = (a + half * (GRID - HALF_BINS)) * PLANE
            contributions[first : first + PLANE, half * LANES : (half + 1) * LANES] = plane * per_total

        half_grids(mixed, tents, anchors, spread, packed, take)

    regions = lax.broadcasted_iota(jnp.int32, (REGIONS, LANES), 0)
    own_member = jnp.where(regions == infos[2], 1.0, 0.0)
    partner_member = jnp.where((regions == partner_info[2]) & has_partner, 1.0, 0.0)
    members = jnp.concatenate([own_member, partner_member], axis=1).astype(jnp.bfloat16)
    high, low = split_two(contributions[...])
    sums = dot_nt(members, high) + dot_nt(members, low)
    early, late = sums[0 : REGIONS // 2], sums[REGIONS // 2 :]
    kept_sums[...] = jnp.where(odd_slab, late, early)
    sent_sums[...] = jnp.where(odd_slab, early, late)


def grid_kernel(half, rows, mixer, edge_fields, inner_fields, tents, grids, field, spread, packed):
    clear_tail(packed)
    total = field.shape[0]
    quarter = edge_fields.shape[1] // 2
    for k in range(2):
        field[0:quarter] = edge_fields[k, 0:quarter]
        field[quarter : total - quarter] = inner_fields[k]
        field[total - quarter :] = edge_fields[k, quarter:]
        mixed = dot(mixer[half], field[...]).astype(jnp.bfloat16)

        def take(a, plane):
            grids[k, a * PLANE : (a + 1) * PLANE, :] = plane.astype(grids.dtype)

        half_grids(mixed, tents, rows[half], spread, packed, take)


def strong_kernel(edge_strong, inner_strong, strong, rows):
    rows[0:4] = edge_strong[0:4]
    rows[4 : rows.shape[0] - 4] = inner_strong[...]
    rows[rows.shape[0] - 4 :] = edge_strong[4:]
    strong[...] = jnp.transpose(rows[...], (1, 0, 2)).astype(jnp.bfloat16)


def all_regions(own_half, other_half):
    early = jnp.where(parity("frame"), other_half[...], own_half[...])
    late = jnp.where(parity("frame"), own_half[...], other_half[...])
    return jnp.concatenate([early, late], axis=0)


def fit_kernel(own_half, other_half, region, slots, lower_grids, upper_grids, estimates, signal, back, chosen):
    sums = all_regions(own_half, other_half)
    profile = sums / jnp.sum(sums, axis=1, keepdims=True)
    regions = lax.broadcasted_iota(jnp.int32, (REGIONS, LANES), 0)
    member = jnp.where(regions == region[...], 1.0, 0.0).astype(jnp.bfloat16)
    high, low = split_two(jnp.transpose(profile, (1, 0))[0:FULL_ROWS])
    chosen[...] = dot(high, member) + dot(low, member)
    join = HALF_ROWS - PLANE
    has_following = lax.axis_index("frame") < lax.axis_size("frame") - 1
    estimate = jnp.zeros((8, LANES), jnp.float32)
    for field, target in ((0, signal), (1, back)):
        upper = jnp.where(has_following, upper_grids[field].astype(jnp.float32), 0.0)
        for r in range(0, FULL_ROWS, 8):
            value = lower_grids[field, r : r + 8] if r < HALF_ROWS else None
            if r >= join:
                late = upper[r - join : r - join + 8]
                value = late if value is None else value + late
            if field == 0:
                estimate = estimate + value
            target[r : r + 8] = value if field == 0 else value + 1.0
    estimate = jnp.sum(estimate, axis=0, keepdims=True)
    for _ in range(ITERS):
        level = jnp.broadcast_to(jnp.maximum(estimate, 0.0), (8, LANES))
        sums_up = [jnp.zeros((8, LANES), jnp.float32)] * 2
        sums_low = [jnp.zeros((8, LANES), jnp.float32)] * 2
        for r in range(0, FULL_ROWS, 8):
            share = chosen[r : r + 8]
            ratio = share / (back[r : r + 8] + level * share)
            k = r // 8 % 2
            sums_up[k] = sums_up[k] + ratio * signal[r : r + 8]
            sums_low[k] = sums_low[k] + ratio * share
        upper_sum = jnp.sum(sums_up[0] + sums_up[1], axis=0, keepdims=True)
        lower_sum = jnp.sum(sums_low[0] + sums_low[1], axis=0, keepdims=True)
        estimate = upper_sum / lower_sum
    devices = estimates.shape[0]
    target = lax.broadcasted_iota(jnp.int32, (devices, LANES), 0) * 2
    for j in range(2):
        held = jnp.where(slots[...] == target + j, estimate, 0.0)
        estimates[:, j : j + 1] = jnp.sum(held, axis=1, keepdims=True)


def profile_kernel(own_half, other_half, profiles):
    sums = all_regions(own_half, other_half)
    profile = sums / jnp.sum(sums, axis=1, keepdims=True)
    profiles[...] = jnp.concatenate(
        [profile[:, a * PLANE : a * PLANE + GRID * GRID] for a in range(GRID)], axis=1
    )


def spread_kernel(arrived, intensity):
    devices = arrived.shape[0]
    lane = lax.broadcasted_iota(jnp.int32, (devices, 2 * devices), 1)
    source = lax.broadcasted_iota(jnp.int32, (devices, 2 * devices), 0)
    placed = jnp.where(lane == 2 * source, arrived[:, 0:1], 0.0)
    placed = placed + jnp.where(lane == 2 * source + 1, arrived[:, 1:2], 0.0)
    intensity[...] = jnp.sum(placed, axis=0, keepdims=True)


def slot_numbers(owners):
    position = jnp.arange(owners.shape[0], dtype=jnp.int32)
    earlier = (owners[None, :] == owners[:, None]) & (position[None, :] < position[:, None])
    return owners * 2 + jnp.sum(jnp.where(earlier, 1, 0), axis=1).astype(jnp.int32)


def pairs_even(count):
    return [(i, i ^ 1) for i in range(count)]


def pairs_odd(count):
    inner = [(i, i + 1 if i % 2 else i - 1) for i in range(1, count - 1)]
    return [(0, 0)] + inner + [(count - 1, count - 1)]


def swapped(x, axis, flip):
    return lax.ppermute(x, axis, [(i, i ^ flip) for i in range(lax.axis_size(axis))])


def summed_over_four(sums, axis, flips):
    sent = sums.astype(jnp.bfloat16)
    one, two, three = [swapped(sent, axis, flip).astype(jnp.float32) for flip in flips]
    return (sent.astype(jnp.float32) + one) + (two + three)


def per_device(image, gain, pixel_mask, anchor_row, anchor_col, owner, region):
    frames, height, columns = image.shape
    slabs = lax.axis_size("frame")
    bands = lax.axis_size("refl")
    devices = slabs * bands
    f32, bf16 = jnp.float32, jnp.bfloat16
    vmem = pl.BlockSpec(memory_space=pltpu.VMEM)

    def shape(dims, dtype=f32):
        return jax.ShapeDtypeStruct(dims, dtype)

    def call(kernel, operands, outs, scratch=(), name=None, work=1):
        return pl.pallas_call(
            kernel,
            in_specs=[vmem] * len(operands),
            out_specs=[vmem] * len(outs),
            out_shape=outs,
            scratch_shapes=[pltpu.VMEM(s.shape, s.dtype) for s in scratch],
            compiler_params=PARAMS,
            cost_estimate=pl.CostEstimate(flops=work, bytes_accessed=work, transcendentals=0),
            name=name,
        )(*operands)

    row, column, area = (x.reshape(1, -1) for x in (anchor_row, anchor_col, region))
    first, second, core, chip, kept = pl.pallas_call(
        send_kernel,
        in_specs=[pl.BlockSpec(memory_space=pl.ANY)] * 6,
        out_specs=[vmem] * 5,
        out_shape=[shape((HALO + 1, frames, columns))] * 2
        + [shape((height + 8, columns))] * 2
        + [shape((height + 1 + 3 * height // 8, frames, columns))],
        scratch_shapes=[
            pltpu.VMEM((frames, height, columns), f32),
            pltpu.VMEM((height, columns), f32),
            pltpu.VMEM((height, columns), jnp.int32),
            pltpu.VMEM((3, 1, LANES), jnp.int32),
            pltpu.SemaphoreType.DMA((6,)),
        ],
        name="sent",
    )(image, gain, pixel_mask, row, column, area)
    halo_second = lax.ppermute(second, "refl", pairs_odd(bands))
    halo_first = lax.ppermute(first, "refl", pairs_even(bands))
    from_core = lax.ppermute(core, "frame", pairs_even(slabs))
    from_chip = lax.ppermute(chip, "frame", pairs_odd(slabs))
    slots = slot_numbers(owner[:, 0])[None, :]

    inner = height - 8
    tent_shape = shape((columns, GRID * LANES), bf16)
    inner_strong, inner_fields, own_tents = call(
        inner_kernel,
        (kept,),
        [shape((inner, frames, columns)), shape((3, inner * frames, columns), bf16), tent_shape],
        [shape((height, columns)), shape((3, inner, columns))],
        name="inner",
    )

    mixer = jnp.asarray(depth_mixer(height, frames), bf16)
    field_shape = shape((height * frames, columns), bf16)
    spread_shape = shape((2, height * 8, 2 * LANES))
    packed_shape = shape((PLANE * 8, LANES))
    edge_strong, edge_fields, partner_tents, rows, kept_sums, sent_sums = call(
        spot_kernel,
        (
            kept,
            halo_first,
            halo_second,
            from_core,
            from_chip,
            mixer,
            inner_fields,
            own_tents,
        ),
        [
            shape((8, frames, columns)),
            shape((3, 8 * frames, columns), bf16),
            tent_shape,
            shape((2, 1, LANES), jnp.int32),
            shape((REGIONS // 2, WIDE_ROWS)),
            shape((REGIONS // 2, WIDE_ROWS)),
        ],
        [
            shape((2 * (HALO + 4 + HALO), frames, columns)),
            shape((height, columns)),
            shape((3, 16, columns)),
            field_shape,
            spread_shape,
            packed_shape,
            shape((WIDE_ROWS, 2 * LANES)),
        ],
        name="spots",
    )
    sums = kept_sums + swapped(sent_sums, "frame", 1)
    sums, edge_fields = lax.optimization_barrier((sums, edge_fields))
    scratch = [field_shape, spread_shape, packed_shape]
    (upper_grids,) = call(
        functools.partial(grid_kernel, 1),
        (rows, mixer, edge_fields, inner_fields, partner_tents),
        [shape((2, HALF_ROWS, LANES), bf16)],
        scratch,
        name="upper",
    )
    sums = summed_over_four(sums, "refl", (1, 2, 3))
    sums, upper_grids, edge_fields = lax.optimization_barrier((sums, upper_grids, edge_fields))
    upper_grids = lax.ppermute(upper_grids, "frame", [((i + 1) % slabs, i) for i in range(slabs)])
    (lower_grids,) = call(
        functools.partial(grid_kernel, 0),
        (rows, mixer, edge_fields, inner_fields, own_tents),
        [shape((2, HALF_ROWS, LANES))],
        scratch,
        name="lower",
    )
    sums = summed_over_four(sums, "refl", (4, 8, 12))
    sums, lower_grids = lax.optimization_barrier((sums, lower_grids))
    sums = summed_over_four(sums, "frame", (2, 4, 6))
    other = swapped(sums, "frame", 1)
    (strong,) = call(
        strong_kernel,
        (edge_strong, inner_strong),
        [shape((frames, height, columns), bf16)],
        [shape((height, frames, columns))],
        name="strong",
    )
    (estimates,) = call(
        fit_kernel,
        (sums, other, area, slots, lower_grids, upper_grids),
        [shape((devices, 2))],
        [shape((FULL_ROWS, LANES))] * 3,
        name="fit",
    )
    arrived = lax.all_to_all(estimates, ("frame", "refl"), split_axis=0, concat_axis=0, tiled=True)
    (profiles,) = call(profile_kernel, (sums, other), [shape((REGIONS, GRID * GRID * GRID))], name="profiles")
    (intensity,) = call(spread_kernel, (arrived,), [shape((1, devices * 2))], name="intensity")
    return (strong, intensity, profiles)


def solution(mesh):
    in_specs = (
        P("frame", "refl", None),
        P("refl", None),
        P("refl", None),
        P(("frame", "refl")),
        P(("frame", "refl")),
        P(("frame", "refl"), None),
        P(("frame", "refl"), None),
    )
    out_specs = (P("frame", "refl", None), P(("frame", "refl"), None), P())
    return jax.shard_map(
        per_device, mesh=mesh, in_specs=in_specs, out_specs=out_specs, check_vma=False
    )
```

```python
import functools

import jax
import jax.numpy as jnp
import numpy as np
from jax import lax
from jax.experimental import pallas as pl
from jax.experimental.pallas import tpu as pltpu
from jax.sharding import PartitionSpec as P

SB_EDGE = 16
GRID = 9
REGIONS = 32
ITERS = 3
HALO = 3
LANES = 128
HALF_BINS = 5
PLANE = 88
HALF_ROWS = HALF_BINS * PLANE
FULL_ROWS = GRID * PLANE
WIDE_ROWS = 896
PARAMS = pltpu.CompilerParams(vmem_limit_bytes=24 * 1024 * 1024)


def tent_values():
    centres = (np.arange(SB_EDGE, dtype=np.float32) + 0.5) * (GRID / SB_EDGE)
    bins = np.arange(GRID, dtype=np.float32) + 0.5
    return np.maximum(0.0, 1.0 - np.abs(centres[None, :] - bins[:, None]))


TENT = tent_values()
EDGE_WEIGHT = TENT.sum(axis=0)


def depth_mixer(rows, frames):
    mixer = np.zeros((2, rows, 8, rows, frames), np.float32)
    for row in range(rows):
        mixer[0, row, :HALF_BINS, row, :] = TENT[:HALF_BINS, :frames]
        mixer[1, row, :HALF_BINS, row, :] = TENT[GRID - HALF_BINS :, frames:]
    return mixer.reshape(2, rows * 8, rows * frames)


def dot(a, b):
    return lax.dot_general(a, b, (((1,), (0,)), ((), ())), preferred_element_type=jnp.float32)


def dot_nt(a, b):
    return lax.dot_general(a, b, (((1,), (1,)), ((), ())), preferred_element_type=jnp.float32)


def split_two(x):
    high = x.astype(jnp.bfloat16)
    return high, (x - high.astype(jnp.float32)).astype(jnp.bfloat16)


def parity(axis):
    return lax.axis_index(axis) % 2 == 1


def send_kernel(
    image,
    gain,
    mask,
    row,
    column,
    region,
    first,
    second,
    core,
    chip,
    kept,
    counts_in,
    gains,
    masks,
    infos,
    arrived,
):
    frames, height, columns = image.shape
    odd_band = parity("refl")
    odd_slab = parity("frame")
    copies = [(image, counts_in), (gain, gains), (mask, masks)]
    copies += [(info, infos.at[k]) for k, info in enumerate((row, column, region))]
    copies = [pltpu.make_async_copy(*copy, arrived.at[k]) for k, copy in enumerate(copies)]
    for copy in copies:
        copy.start()
    for copy in copies:
        copy.wait()
    live = masks[...].astype(jnp.float32)
    values = counts_in[...] * (gains[...] * live)[None]
    kept[0:height] = jnp.transpose(values, (1, 0, 2))

    head, tail = kept[0:HALO], kept[height - HALO : height]
    first[0:HALO] = jnp.where(odd_band, head, tail)
    second[0:HALO] = jnp.where(odd_band, tail, head)
    head, tail = live[0:HALO], live[height - HALO :]
    first[HALO, 0:HALO] = jnp.where(odd_band, head, tail)
    second[HALO, 0:HALO] = jnp.where(odd_band, tail, head)

    counts = values.astype(jnp.bfloat16).astype(jnp.float32)
    inner = counts[1]
    for z in range(2, frames - 1):
        inner = inner + counts[z]
    border = float(EDGE_WEIGHT[0])
    lower = inner + counts[frames - 1] + border * counts[0]
    upper = inner + counts[0] + border * counts[frames - 1]
    core[0:height] = jnp.where(odd_slab, upper, lower)
    chip[0:height] = jnp.where(odd_slab, lower, upper)
    for k in range(3):
        sent = infos[k].astype(jnp.float32)
        core[height + k : height + k + 1, 0:LANES] = sent
        chip[height + k : height + k + 1, 0:LANES] = sent
        kept[height, k : k + 1, 0:LANES] = sent
    for place, whole in enumerate((live, lower, upper)):
        first_row = height + 1 + place * height // 8
        kept[first_row : first_row + height // 8] = whole.reshape(height // 8, 8, columns)


def kept_info(kept, height, k):
    return kept[height, k : k + 1, 0:LANES].astype(jnp.int32)


def kept_rows(kept, height, place):
    first_row = height + 1 + place * height // 8
    return kept[first_row : first_row + height // 8].reshape(height, kept.shape[2])


def shoebox_offsets(anchors, extent):
    return lax.broadcasted_iota(jnp.int32, (extent, LANES), 0) - anchors


def total_weights(anchors, extent):
    offset = shoebox_offsets(anchors, extent)
    inside = (offset >= 0) & (offset < SB_EDGE)
    border = (offset == 0) | (offset == SB_EDGE - 1)
    return jnp.where(border, float(EDGE_WEIGHT[0]), jnp.where(inside, 1.0, 0.0))


def count_totals(levels, row, column):
    height, columns = levels.shape
    high, low = split_two(levels)
    by_column = total_weights(column, columns).astype(jnp.bfloat16)
    sums = dot(high, by_column) + dot(low, by_column)
    return jnp.sum(sums * total_weights(row, height), axis=0, keepdims=True)


def column_tents(column, columns, tents):
    offset = shoebox_offsets(column, columns)
    offset = jnp.where(offset < 0, -2, jnp.where(offset >= SB_EDGE, SB_EDGE + 1, offset))
    centre = (offset.astype(jnp.float32) + 0.5) * (GRID / SB_EDGE) - GRID / 2
    centre = centre.astype(jnp.bfloat16)
    one, zero = jnp.bfloat16(1.0), jnp.bfloat16(0.0)
    for c in range(GRID):
        distance = jnp.abs(centre - jnp.bfloat16(c - GRID // 2))
        tents[:, c * LANES : (c + 1) * LANES] = jnp.maximum(one - distance, zero)


def window_sums(x):
    width = x.shape[-1]
    axis = x.ndim - 1
    pairs = x + pltpu.roll(x, 1, axis)
    fours = pairs + pltpu.roll(pairs, 2, axis)
    return fours + pltpu.roll(fours, width - 3, axis) - x


def window_counts(mask_rows, start, rows, terms, at):
    count = mask_rows[start : start + rows, :]
    for k in range(1, 2 * HALO + 1):
        count = count + mask_rows[start + k : start + k + rows, :]
    columns = count.shape[-1]
    tail = jnp.zeros((rows, LANES), jnp.float32)
    count = window_sums(jnp.concatenate([count, tail], axis=1))[:, 0:columns]
    per_spread = 1.0 / jnp.maximum(count - 1.0, 1.0)
    terms[0, at : at + rows, :] = 1.0 / jnp.maximum(count, 1.0)
    terms[1, at : at + rows, :] = 2.0 * per_spread
    terms[2, at : at + rows, :] = 2.0 + 12.0 * jnp.sqrt(2.0 * per_spread)


def vertical_sums(padded, base):
    rows = [padded[base + k] for k in range(2 * HALO + 2)]
    shared = rows[1]
    for k in range(2, 2 * HALO + 1):
        shared = shared + rows[k]
    squares = [x * x for x in rows]
    shared_square = squares[1]
    for k in range(2, 2 * HALO + 1):
        shared_square = shared_square + squares[k]
    total = jnp.stack([shared + rows[0], shared + rows[-1]])
    square = jnp.stack([shared_square + squares[0], shared_square + squares[-1]])
    return total, square


def row_pair(padded, base, terms, term_row, mask_rows, live_row, fields, slot):
    frames, columns = padded.shape[1:]
    frame_tail = jnp.zeros((2, frames, LANES), jnp.float32)
    total, square = [
        window_sums(jnp.concatenate([x, frame_tail], axis=2))[:, :, 0:columns]
        for x in vertical_sums(padded, base)
    ]
    row_weights(total, square, padded, base, terms, term_row, mask_rows, live_row, fields, slot)


def row_weights(total, square, padded, base, terms, term_row, mask_rows, live_row, fields, slot):
    frames, columns = padded.shape[1:]
    value = jnp.stack([padded[base + HALO], padded[base + HALO + 1]])

    def every_frame(row):
        return jnp.broadcast_to(row, (frames, columns))

    def term(j):
        return jnp.stack([every_frame(terms[j, pl.ds(term_row + k, 1), :]) for k in range(2)])

    live = jnp.stack([every_frame(mask_rows[pl.ds(live_row + k, 1), :]) for k in range(2)])
    background = total * term(0)
    variance = (square - total * background) * term(1)
    per_root = lax.rsqrt(background + 1.0)
    root = background * lax.rsqrt(jnp.maximum(background, 1e-30))
    shortfall = term(2) - variance * (per_root * per_root)
    below = (background - value + 3.0 * root) * per_root
    gates = (1.0 + jnp.exp(shortfall)) * (1.0 + jnp.exp(below))
    weight = pl.reciprocal(gates, approx=True)
    weight = live * (weight * (2.0 - gates * weight))
    flat = (2 * frames, columns)
    weight, value, background = (
        x.reshape(flat).astype(jnp.bfloat16) for x in (weight, value, background)
    )
    at = pl.ds(pl.multiple_of(slot * 2 * frames, 2 * frames), 2 * frames)
    fields[0, at, :] = value - background
    fields[1, at, :] = background
    fields[2, at, :] = weight * value
    fields[3, at, :] = weight


def inner_kernel(kept, fields, tents, live, terms, parts, windows, band):
    height, columns = live.shape
    live[...] = kept_rows(kept, height, 0)
    column_tents(kept_info(kept, height, 1), columns, tents)
    rows = height - 8
    window_counts(live, 1, rows, terms, 0)

    frames = kept.shape[1]
    pairs = rows // 2
    step = 2 * frames

    def down(i, carry):
        at = pl.ds(pl.multiple_of(i * step, step), step)
        for k, x in enumerate(vertical_sums(kept, 2 * i + 1)):
            high, low = split_two(x.reshape(step, columns))
            parts[k, at, 0:columns] = high
            parts[k, at, columns:] = low
        return carry

    def across(i, carry):
        at = pl.ds(pl.multiple_of(i * step, step), step)
        total, square = [windows[k, at, :].reshape(2, frames, columns) for k in range(2)]
        row_weights(total, square, kept, 2 * i + 1, terms, 2 * i, live, 2 * i + 4, fields, i)
        return carry

    shape = (columns, columns)
    apart = lax.broadcasted_iota(jnp.int32, shape, 0) - lax.broadcasted_iota(jnp.int32, shape, 1)
    near = jnp.where(jnp.abs(apart) <= HALO, 1.0, 0.0).astype(jnp.bfloat16)
    band[0:columns] = near
    band[columns:] = near
    lax.fori_loop(0, pairs, down, 0, unroll=6)
    for k in range(2):
        windows[k] = dot(parts[k], band[...])
    lax.fori_loop(0, pairs, across, 0, unroll=6)


def half_grids(mixed, tents, anchors, spread, packed, take):
    height = mixed.shape[0] // 8
    shift = jnp.broadcast_to(anchors, (8, LANES))
    bits = [(shift & (1 << k)) != 0 for k in range(5)]

    def one_column(c, spread, at):
        rows = [spread[8 * r : 8 * r + 8, at] for r in range(height)]
        rows = [
            jnp.where(bits[4], rows[r + 16], rows[r]) if r + 16 < height else rows[r]
            for r in range(31)
        ]
        for k in (3, 2, 1, 0):
            keep = 16 + (1 << k) - 1
            rows = [jnp.where(bits[k], rows[r + (1 << k)], rows[r]) for r in range(keep)]
        for b in range(GRID):
            value = None
            for y in range(SB_EDGE):
                if TENT[b, y] != 0.0:
                    term = rows[y] * float(TENT[b, y])
                    value = term if value is None else value + term
            packed[(b * GRID + c) * 8 : (b * GRID + c) * 8 + 8, :] = value

    for c in range(0, GRID, 2):
        end = min(c + 2, GRID)
        slot = spread.at[c // 2 % 2]
        slot[:, 0 : (end - c) * LANES] = dot(mixed, tents[:, c * LANES : end * LANES])
        for k in range(end - c):
            one_column(c + k, slot, slice(k * LANES, (k + 1) * LANES))
    for a in range(HALF_BINS):
        take(a, packed[pl.ds(a, PLANE, stride=8), :])


def clear_tail(packed):
    used = GRID * GRID * 8
    packed[used:, :] = jnp.zeros((packed.shape[0] - used, LANES), jnp.float32)


def spot_kernel(
    kept,
    halo_first,
    halo_second,
    from_core,
    from_chip,
    mixer,
    inner_fields,
    own_tents,
    edge_fields,
    partner_tents,
    rows,
    kept_sums,
    sent_sums,
    padded,
    mask_rows,
    terms,
    field,
    spread,
    packed,
    contributions,
):
    frames, columns = kept.shape[1:]
    height = field.shape[0] // frames
    odd_band = parity("refl")
    odd_slab = parity("frame")
    has_partner = lax.axis_index("frame") > 0

    halo_a = halo_first[...]
    halo_b = halo_second[0 : HALO + 1]
    band = lax.axis_index("refl")
    before = jnp.where(odd_band, halo_a, jnp.where(band > 0, halo_b, 0.0))
    after = jnp.where(odd_band, jnp.where(band < lax.axis_size("refl") - 1, halo_b, 0.0), halo_a)
    near = 4 + HALO
    padded[0:HALO] = before[0:HALO]
    padded[HALO : HALO + near] = kept[0:near]
    padded[HALO + near : HALO + 2 * near] = kept[height - near : height]
    padded[HALO + 2 * near :] = after[0:HALO]
    live = kept_rows(kept, height, 0)
    mask_rows[8 - HALO : 8, :] = before[HALO, 0:HALO]
    mask_rows[8 : 8 + near, :] = live[0:near]
    mask_rows[24 - HALO : 24 - HALO + near, :] = live[height - near :]
    mask_rows[28:31, :] = after[HALO, 0:HALO]
    window_counts(mask_rows, 5, 4, terms, 0)
    window_counts(mask_rows, 21, 4, terms, 8)
    for slot, (base, term_row, live_row) in enumerate(((0, 0, 8), (2, 2, 10), (10, 8, 24), (12, 10, 26))):
        row_pair(padded, base, terms, term_row, mask_rows, live_row, edge_fields, slot)

    partner = jnp.where(odd_slab, from_core[...], from_chip[...])
    following = jnp.where(odd_slab, from_chip[0:height], from_core[0:height])
    following = jnp.where(lax.axis_index("frame") < lax.axis_size("frame") - 1, following, 0.0)
    lower = kept_rows(kept, height, 1)
    upper = kept_rows(kept, height, 2)
    infos = [kept_info(kept, height, k) for k in range(3)]
    partner_info = [partner[height + k : height + k + 1, 0:LANES].astype(jnp.int32) for k in range(3)]
    rows[0] = infos[0]
    rows[1] = partner_info[0]
    own_total = count_totals(lower + following, infos[0], infos[1])
    partner_total = count_totals(partner[0:height] + upper, partner_info[0], partner_info[1])
    partner_total = jnp.where(has_partner, partner_total, 1.0)
    column_tents(partner_info[1], columns, partner_tents)

    contributions[...] = jnp.zeros(contributions.shape, jnp.float32)
    clear_tail(packed)
    quarter = 4 * frames
    field[0:quarter] = edge_fields[2, 0:quarter]
    field[quarter : height * frames - quarter] = inner_fields[2]
    field[height * frames - quarter :] = edge_fields[2, quarter:]
    for half, (anchors, tents, total) in enumerate(
        ((infos[0], own_tents, own_total), (partner_info[0], partner_tents, partner_total))
    ):
        mixed = dot(mixer[half], field[...]).astype(jnp.bfloat16)
        per_total = 1.0 / total

        def take(a, plane):
            first = (a + half * (GRID - HALF_BINS)) * PLANE
            contributions[first : first + PLANE, half * LANES : (half + 1) * LANES] = plane * per_total

        half_grids(mixed, tents, anchors, spread, packed, take)

    regions = lax.broadcasted_iota(jnp.int32, (REGIONS, LANES), 0)
    own_member = jnp.where(regions == infos[2], 1.0, 0.0)
    partner_member = jnp.where((regions == partner_info[2]) & has_partner, 1.0, 0.0)
    members = jnp.concatenate([own_member, partner_member], axis=1).astype(jnp.bfloat16)
    high, low = split_two(contributions[...])
    sums = dot_nt(members, high) + dot_nt(members, low)
    early, late = sums[0 : REGIONS // 2], sums[REGIONS // 2 :]
    kept_sums[...] = jnp.where(odd_slab, late, early)
    sent_sums[...] = jnp.where(odd_slab, early, late)


def grid_kernel(half, rows, mixer, edge_fields, inner_fields, tents, grids, field, spread, packed):
    clear_tail(packed)
    total = field.shape[0]
    quarter = edge_fields.shape[1] // 2
    for k in range(2):
        field[0:quarter] = edge_fields[k, 0:quarter]
        field[quarter : total - quarter] = inner_fields[k]
        field[total - quarter :] = edge_fields[k, quarter:]
        mixed = dot(mixer[half], field[...]).astype(jnp.bfloat16)

        def take(a, plane):
            grids[k, a * PLANE : (a + 1) * PLANE, :] = plane.astype(grids.dtype)

        half_grids(mixed, tents, rows[half], spread, packed, take)


def strong_kernel(edge_fields, inner_fields, strong):
    frames, height, columns = strong.shape
    quarter = edge_fields.shape[1] // 2
    edges, inner = edge_fields[3].astype(jnp.float32), inner_fields[3].astype(jnp.float32)
    rows = jnp.concatenate([edges[0:quarter], inner, edges[quarter:]], axis=0)
    rows = rows.reshape(height, frames, columns)
    strong[...] = jnp.transpose(rows, (1, 0, 2)).astype(jnp.bfloat16)


def all_regions(own_half, other_half):
    early = jnp.where(parity("frame"), other_half[...], own_half[...])
    late = jnp.where(parity("frame"), own_half[...], other_half[...])
    return jnp.concatenate([early, late], axis=0)


def fit_kernel(own_half, other_half, region, slots, lower_grids, upper_grids, estimates, signal, back, chosen):
    sums = all_regions(own_half, other_half)
    profile = sums / jnp.sum(sums, axis=1, keepdims=True)
    regions = lax.broadcasted_iota(jnp.int32, (REGIONS, LANES), 0)
    member = jnp.where(regions == region[...], 1.0, 0.0).astype(jnp.bfloat16)
    high, low = split_two(jnp.transpose(profile, (1, 0))[0:FULL_ROWS])
    chosen[...] = dot(high, member) + dot(low, member)
    join = HALF_ROWS - PLANE
    has_following = lax.axis_index("frame") < lax.axis_size("frame") - 1
    estimate = jnp.zeros((8, LANES), jnp.float32)
    for field, target in ((0, signal), (1, back)):
        upper = jnp.where(has_following, upper_grids[field].astype(jnp.float32), 0.0)
        for r in range(0, FULL_ROWS, 8):
            value = lower_grids[field, r : r + 8] if r < HALF_ROWS else None
            if r >= join:
                late = upper[r - join : r - join + 8]
                value = late if value is None else value + late
            if field == 0:
                estimate = estimate + value
            target[r : r + 8] = value if field == 0 else value + 1.0
    estimate = jnp.sum(estimate, axis=0, keepdims=True)
    for _ in range(ITERS):
        level = jnp.broadcast_to(jnp.maximum(estimate, 0.0), (8, LANES))
        sums_up = [jnp.zeros((8, LANES), jnp.float32)] * 2
        sums_low = [jnp.zeros((8, LANES), jnp.float32)] * 2
        for r in range(0, FULL_ROWS, 8):
            share = chosen[r : r + 8]
            ratio = share / (back[r : r + 8] + level * share)
            k = r // 8 % 2
            sums_up[k] = sums_up[k] + ratio * signal[r : r + 8]
            sums_low[k] = sums_low[k] + ratio * share
        upper_sum = jnp.sum(sums_up[0] + sums_up[1], axis=0, keepdims=True)
        lower_sum = jnp.sum(sums_low[0] + sums_low[1], axis=0, keepdims=True)
        estimate = upper_sum / lower_sum
    devices = estimates.shape[0]
    target = lax.broadcasted_iota(jnp.int32, (devices, LANES), 0) * 2
    for j in range(2):
        held = jnp.where(slots[...] == target + j, estimate, 0.0)
        estimates[:, j : j + 1] = jnp.sum(held, axis=1, keepdims=True)


def profile_kernel(own_half, other_half, profiles):
    sums = all_regions(own_half, other_half)
    profile = sums / jnp.sum(sums, axis=1, keepdims=True)
    profiles[...] = jnp.concatenate(
        [profile[:, a * PLANE : a * PLANE + GRID * GRID] for a in range(GRID)], axis=1
    )


def spread_kernel(arrived, intensity):
    devices = arrived.shape[0]
    lane = lax.broadcasted_iota(jnp.int32, (devices, 2 * devices), 1)
    source = lax.broadcasted_iota(jnp.int32, (devices, 2 * devices), 0)
    placed = jnp.where(lane == 2 * source, arrived[:, 0:1], 0.0)
    placed = placed + jnp.where(lane == 2 * source + 1, arrived[:, 1:2], 0.0)
    intensity[...] = jnp.sum(placed, axis=0, keepdims=True)


def slot_numbers(owners):
    position = jnp.arange(owners.shape[0], dtype=jnp.int32)
    earlier = (owners[None, :] == owners[:, None]) & (position[None, :] < position[:, None])
    return owners * 2 + jnp.sum(jnp.where(earlier, 1, 0), axis=1).astype(jnp.int32)


def pairs_even(count):
    return [(i, i ^ 1) for i in range(count)]


def pairs_odd(count):
    inner = [(i, i + 1 if i % 2 else i - 1) for i in range(1, count - 1)]
    return [(0, 0)] + inner + [(count - 1, count - 1)]


def swapped(x, axis, flip):
    return lax.ppermute(x, axis, [(i, i ^ flip) for i in range(lax.axis_size(axis))])


def summed_over_four(sums, axis, flips):
    sent = sums.astype(jnp.bfloat16)
    one, two, three = [swapped(sent, axis, flip).astype(jnp.float32) for flip in flips]
    return (sent.astype(jnp.float32) + one) + (two + three)


def per_device(image, gain, pixel_mask, anchor_row, anchor_col, owner, region):
    frames, height, columns = image.shape
    slabs = lax.axis_size("frame")
    bands = lax.axis_size("refl")
    devices = slabs * bands
    f32, bf16 = jnp.float32, jnp.bfloat16
    vmem = pl.BlockSpec(memory_space=pltpu.VMEM)

    def shape(dims, dtype=f32):
        return jax.ShapeDtypeStruct(dims, dtype)

    def call(kernel, operands, outs, scratch=(), name=None, work=1):
        return pl.pallas_call(
            kernel,
            in_specs=[vmem] * len(operands),
            out_specs=[vmem] * len(outs),
            out_shape=outs,
            scratch_shapes=[pltpu.VMEM(s.shape, s.dtype) for s in scratch],
            compiler_params=PARAMS,
            cost_estimate=pl.CostEstimate(flops=work, bytes_accessed=work, transcendentals=0),
            name=name,
        )(*operands)

    row, column, area = (x.reshape(1, -1) for x in (anchor_row, anchor_col, region))
    first, second, core, chip, kept = pl.pallas_call(
        send_kernel,
        in_specs=[pl.BlockSpec(memory_space=pl.ANY)] * 6,
        out_specs=[vmem] * 5,
        out_shape=[shape((HALO + 1, frames, columns)), shape((HALO + 3, frames, columns))]
        + [shape((height + 8, columns))] * 2
        + [shape((height + 1 + 3 * height // 8, frames, columns))],
        scratch_shapes=[
            pltpu.VMEM((frames, height, columns), f32),
            pltpu.VMEM((height, columns), f32),
            pltpu.VMEM((height, columns), jnp.int32),
            pltpu.VMEM((3, 1, LANES), jnp.int32),
            pltpu.SemaphoreType.DMA((6,)),
        ],
        name="sent",
    )(image, gain, pixel_mask, row, column, area)
    halo_second = lax.ppermute(second, "refl", pairs_odd(bands))
    halo_first = lax.ppermute(first, "refl", pairs_even(bands))
    from_core = lax.ppermute(core, "frame", pairs_even(slabs))
    from_chip = lax.ppermute(chip, "frame", pairs_odd(slabs))
    slots = slot_numbers(owner[:, 0])[None, :]

    inner = height - 8
    tent_shape = shape((columns, GRID * LANES), bf16)
    inner_fields, own_tents = call(
        inner_kernel,
        (kept,),
        [shape((4, inner * frames, columns), bf16), tent_shape],
        [
            shape((height, columns)),
            shape((3, inner, columns)),
            shape((2, inner * frames, 2 * columns), bf16),
            shape((2, inner * frames, columns)),
            shape((2 * columns, columns), bf16),
        ],
        name="inner",
    )

    mixer = jnp.asarray(depth_mixer(height, frames), bf16)
    field_shape = shape((height * frames, columns), bf16)
    spread_shape = shape((2, height * 8, 2 * LANES))
    packed_shape = shape((PLANE * 8, LANES))
    edge_fields, partner_tents, rows, kept_sums, sent_sums = call(
        spot_kernel,
        (
            kept,
            halo_first,
            halo_second,
            from_core,
            from_chip,
            mixer,
            inner_fields,
            own_tents,
        ),
        [
            shape((4, 8 * frames, columns), bf16),
            tent_shape,
            shape((2, 1, LANES), jnp.int32),
            shape((REGIONS // 2, WIDE_ROWS)),
            shape((REGIONS // 2, WIDE_ROWS)),
        ],
        [
            shape((2 * (HALO + 4 + HALO), frames, columns)),
            shape((height, columns)),
            shape((3, 16, columns)),
            field_shape,
            spread_shape,
            packed_shape,
            shape((WIDE_ROWS, 2 * LANES)),
        ],
        name="spots",
    )
    sums = kept_sums + swapped(sent_sums, "frame", 1)
    sums, edge_fields = lax.optimization_barrier((sums, edge_fields))
    scratch = [field_shape, spread_shape, packed_shape]
    (upper_grids,) = call(
        functools.partial(grid_kernel, 1),
        (rows, mixer, edge_fields, inner_fields, partner_tents),
        [shape((2, HALF_ROWS, LANES), bf16)],
        scratch,
        name="upper",
    )
    sums = summed_over_four(sums, "refl", (1, 2, 3))
    sums, upper_grids, edge_fields = lax.optimization_barrier((sums, upper_grids, edge_fields))
    upper_grids = lax.ppermute(upper_grids, "frame", [((i + 1) % slabs, i) for i in range(slabs)])
    (lower_grids,) = call(
        functools.partial(grid_kernel, 0),
        (rows, mixer, edge_fields, inner_fields, own_tents),
        [shape((2, HALF_ROWS, LANES))],
        scratch,
        name="lower",
    )
    sums = summed_over_four(sums, "refl", (4, 8, 12))
    sums, lower_grids = lax.optimization_barrier((sums, lower_grids))
    sums = summed_over_four(sums, "frame", (2, 4, 6))
    other = swapped(sums, "frame", 1)
    (strong,) = call(
        strong_kernel,
        (edge_fields, inner_fields),
        [shape((frames, height, columns), bf16)],
        name="strong",
    )
    (estimates,) = call(
        fit_kernel,
        (sums, other, area, slots, lower_grids, upper_grids),
        [shape((devices, 2))],
        [shape((FULL_ROWS, LANES))] * 3,
        name="fit",
    )
    arrived = lax.all_to_all(estimates, ("frame", "refl"), split_axis=0, concat_axis=0, tiled=True)
    (profiles,) = call(profile_kernel, (sums, other), [shape((REGIONS, GRID * GRID * GRID))], name="profiles")
    (intensity,) = call(spread_kernel, (arrived,), [shape((1, devices * 2))], name="intensity")
    return (strong, intensity, profiles)


def solution(mesh):
    in_specs = (
        P("frame", "refl", None),
        P("refl", None),
        P("refl", None),
        P(("frame", "refl")),
        P(("frame", "refl")),
        P(("frame", "refl"), None),
        P(("frame", "refl"), None),
    )
    out_specs = (P("frame", "refl", None), P(("frame", "refl"), None), P())
    return jax.shard_map(
        per_device, mesh=mesh, in_specs=in_specs, out_specs=out_specs, check_vma=False
    )
```

```python
import functools

import jax
import jax.numpy as jnp
import numpy as np
from jax import lax
from jax.experimental import pallas as pl
from jax.experimental.pallas import tpu as pltpu
from jax.sharding import PartitionSpec as P

SB_EDGE = 16
GRID = 9
REGIONS = 32
ITERS = 3
HALO = 3
LANES = 128
HALF_BINS = 5
PLANE = 88
HALF_ROWS = HALF_BINS * PLANE
FULL_ROWS = GRID * PLANE
WIDE_ROWS = 896
PARAMS = pltpu.CompilerParams(vmem_limit_bytes=24 * 1024 * 1024)


def tent_values():
    centres = (np.arange(SB_EDGE, dtype=np.float32) + 0.5) * (GRID / SB_EDGE)
    bins = np.arange(GRID, dtype=np.float32) + 0.5
    return np.maximum(0.0, 1.0 - np.abs(centres[None, :] - bins[:, None]))


TENT = tent_values()
EDGE_WEIGHT = TENT.sum(axis=0)


def depth_mixer(rows, frames):
    mixer = np.zeros((2, rows, 8, rows, frames), np.float32)
    for row in range(rows):
        mixer[0, row, :HALF_BINS, row, :] = TENT[:HALF_BINS, :frames]
        mixer[1, row, :HALF_BINS, row, :] = TENT[GRID - HALF_BINS :, frames:]
    return mixer.reshape(2, rows * 8, rows * frames)


def dot(a, b):
    return lax.dot_general(a, b, (((1,), (0,)), ((), ())), preferred_element_type=jnp.float32)


def dot_nt(a, b):
    return lax.dot_general(a, b, (((1,), (1,)), ((), ())), preferred_element_type=jnp.float32)


def split_two(x):
    high = x.astype(jnp.bfloat16)
    return high, (x - high.astype(jnp.float32)).astype(jnp.bfloat16)


def parity(axis):
    return lax.axis_index(axis) % 2 == 1


def send_kernel(
    image,
    gain,
    mask,
    row,
    column,
    region,
    first,
    second,
    core,
    chip,
    kept,
    counts_in,
    gains,
    masks,
    infos,
    arrived,
):
    frames, height, columns = image.shape
    odd_band = parity("refl")
    odd_slab = parity("frame")
    copies = [(image, counts_in), (gain, gains), (mask, masks)]
    copies += [(info, infos.at[k]) for k, info in enumerate((row, column, region))]
    copies = [pltpu.make_async_copy(*copy, arrived.at[k]) for k, copy in enumerate(copies)]
    for copy in copies:
        copy.start()
    for copy in copies:
        copy.wait()
    live = masks[...].astype(jnp.float32)
    values = counts_in[...] * (gains[...] * live)[None]
    kept[0:height] = jnp.transpose(values, (1, 0, 2))

    head, tail = kept[0:HALO], kept[height - HALO : height]
    first[0:HALO] = jnp.where(odd_band, head, tail)
    second[0:HALO] = jnp.where(odd_band, tail, head)
    head, tail = live[0:HALO], live[height - HALO :]
    first[HALO, 0:HALO] = jnp.where(odd_band, head, tail)
    second[HALO, 0:HALO] = jnp.where(odd_band, tail, head)

    counts = values.astype(jnp.bfloat16).astype(jnp.float32)
    inner = counts[1]
    for z in range(2, frames - 1):
        inner = inner + counts[z]
    border = float(EDGE_WEIGHT[0])
    lower = inner + counts[frames - 1] + border * counts[0]
    upper = inner + counts[0] + border * counts[frames - 1]
    core[0:height] = jnp.where(odd_slab, upper, lower)
    chip[0:height] = jnp.where(odd_slab, lower, upper)
    for k in range(3):
        sent = infos[k].astype(jnp.float32)
        core[height + k : height + k + 1, 0:LANES] = sent
        chip[height + k : height + k + 1, 0:LANES] = sent
        kept[height, k : k + 1, 0:LANES] = sent
    for place, whole in enumerate((live, lower, upper)):
        first_row = height + 1 + place * height // 8
        kept[first_row : first_row + height // 8] = whole.reshape(height // 8, 8, columns)


def kept_info(kept, height, k):
    return kept[height, k : k + 1, 0:LANES].astype(jnp.int32)


def kept_rows(kept, height, place):
    first_row = height + 1 + place * height // 8
    return kept[first_row : first_row + height // 8].reshape(height, kept.shape[2])


def shoebox_offsets(anchors, extent):
    return lax.broadcasted_iota(jnp.int32, (extent, LANES), 0) - anchors


def total_weights(anchors, extent):
    offset = shoebox_offsets(anchors, extent)
    inside = (offset >= 0) & (offset < SB_EDGE)
    border = (offset == 0) | (offset == SB_EDGE - 1)
    return jnp.where(border, float(EDGE_WEIGHT[0]), jnp.where(inside, 1.0, 0.0))


def count_totals(levels, row, column):
    height, columns = levels.shape
    high, low = split_two(levels)
    by_column = total_weights(column, columns).astype(jnp.bfloat16)
    sums = dot(high, by_column) + dot(low, by_column)
    return jnp.sum(sums * total_weights(row, height), axis=0, keepdims=True)


def column_tents(column, columns, tents):
    offset = shoebox_offsets(column, columns)
    offset = jnp.where(offset < 0, -2, jnp.where(offset >= SB_EDGE, SB_EDGE + 1, offset))
    centre = (offset.astype(jnp.float32) + 0.5) * (GRID / SB_EDGE) - GRID / 2
    centre = centre.astype(jnp.bfloat16)
    one, zero = jnp.bfloat16(1.0), jnp.bfloat16(0.0)
    for c in range(GRID):
        distance = jnp.abs(centre - jnp.bfloat16(c - GRID // 2))
        tents[:, c * LANES : (c + 1) * LANES] = jnp.maximum(one - distance, zero)


def window_sums(x):
    width = x.shape[-1]
    axis = x.ndim - 1
    pairs = x + pltpu.roll(x, 1, axis)
    fours = pairs + pltpu.roll(pairs, 2, axis)
    return fours + pltpu.roll(fours, width - 3, axis) - x


def window_counts(mask_rows, start, rows, terms, at):
    count = mask_rows[start : start + rows, :]
    for k in range(1, 2 * HALO + 1):
        count = count + mask_rows[start + k : start + k + rows, :]
    columns = count.shape[-1]
    tail = jnp.zeros((rows, LANES), jnp.float32)
    count = window_sums(jnp.concatenate([count, tail], axis=1))[:, 0:columns]
    per_spread = 1.0 / jnp.maximum(count - 1.0, 1.0)
    terms[0, at : at + rows, :] = 1.0 / jnp.maximum(count, 1.0)
    terms[1, at : at + rows, :] = 2.0 * per_spread
    terms[2, at : at + rows, :] = 2.0 + 12.0 * jnp.sqrt(2.0 * per_spread)


def row_pair(padded, base, terms, term_row, mask_rows, live_row, strong_rows, fields, slot):
    frames, columns = padded.shape[1:]
    rows = [padded[base + k] for k in range(2 * HALO + 2)]
    shared = rows[1]
    for k in range(2, 2 * HALO + 1):
        shared = shared + rows[k]
    squares = [x * x for x in rows]
    shared_square = squares[1]
    for k in range(2, 2 * HALO + 1):
        shared_square = shared_square + squares[k]
    frame_tail = jnp.zeros((2, frames, LANES), jnp.float32)
    total = jnp.stack([shared + rows[0], shared + rows[-1]])
    square = jnp.stack([shared_square + squares[0], shared_square + squares[-1]])
    total = window_sums(jnp.concatenate([total, frame_tail], axis=2))[:, :, 0:columns]
    square = window_sums(jnp.concatenate([square, frame_tail], axis=2))[:, :, 0:columns]
    value = jnp.stack([rows[HALO], rows[HALO + 1]])

    def every_frame(row):
        return jnp.broadcast_to(row, (frames, columns))

    def term(j):
        return jnp.stack([every_frame(terms[j, pl.ds(term_row + k, 1), :]) for k in range(2)])

    live = jnp.stack([every_frame(mask_rows[pl.ds(live_row + k, 1), :]) for k in range(2)])
    background = total * term(0)
    variance = (square - total * background) * term(1)
    per_root = lax.rsqrt(background + 1.0)
    root = background * lax.rsqrt(jnp.maximum(background, 1e-30))
    shortfall = term(2) - variance * (per_root * per_root)
    below = (background - value + 3.0 * root) * per_root
    gates = (1.0 + jnp.exp(shortfall)) * (1.0 + jnp.exp(below))
    weight = pl.reciprocal(gates, approx=True)
    weight = live * (weight * (2.0 - gates * weight))
    weight_b = weight.astype(jnp.bfloat16).astype(jnp.float32)
    value_b = value.astype(jnp.bfloat16).astype(jnp.float32)
    background_b = background.astype(jnp.bfloat16).astype(jnp.float32)
    strong_rows[pl.ds(2 * slot, 2)] = weight_b
    at = pl.ds(pl.multiple_of(slot * 2 * frames, 2 * frames), 2 * frames)
    flat = (2 * frames, columns)
    fields[0, at, :] = (value_b - background_b).reshape(flat).astype(jnp.bfloat16)
    fields[1, at, :] = background_b.reshape(flat).astype(jnp.bfloat16)
    fields[2, at, :] = (weight_b * value_b).reshape(flat).astype(jnp.bfloat16)


def inner_kernel(kept, strong_rows, fields, tents, live, terms):
    height, columns = live.shape
    live[...] = kept_rows(kept, height, 0)
    column_tents(kept_info(kept, height, 1), columns, tents)
    rows = height - 8
    window_counts(live, 1, rows, terms, 0)

    def pair(i, carry):
        row_pair(kept, 2 * i + 1, terms, 2 * i, live, 2 * i + 4, strong_rows, fields, i)
        return carry

    lax.fori_loop(0, rows // 2, pair, 0, unroll=6)


def half_grids(mixed, tents, anchors, spread, packed, take):
    height = mixed.shape[0] // 8
    shift = jnp.broadcast_to(anchors, (8, LANES))
    bits = [(shift & (1 << k)) != 0 for k in range(5)]

    def one_column(c, spread, at):
        rows = [spread[8 * r : 8 * r + 8, at] for r in range(height)]
        rows = [
            jnp.where(bits[4], rows[r + 16], rows[r]) if r + 16 < height else rows[r]
            for r in range(31)
        ]
        for k in (3, 2, 1, 0):
            keep = 16 + (1 << k) - 1
            rows = [jnp.where(bits[k], rows[r + (1 << k)], rows[r]) for r in range(keep)]
        for b in range(GRID):
            value = None
            for y in range(SB_EDGE):
                if TENT[b, y] != 0.0:
                    term = rows[y] * float(TENT[b, y])
                    value = term if value is None else value + term
            packed[(b * GRID + c) * 8 : (b * GRID + c) * 8 + 8, :] = value

    for c in range(0, GRID, 2):
        end = min(c + 2, GRID)
        slot = spread.at[c // 2 % 2]
        slot[:, 0 : (end - c) * LANES] = dot(mixed, tents[:, c * LANES : end * LANES])
        for k in range(end - c):
            one_column(c + k, slot, slice(k * LANES, (k + 1) * LANES))
    for a in range(HALF_BINS):
        take(a, packed[pl.ds(a, PLANE, stride=8), :])


def clear_tail(packed):
    used = GRID * GRID * 8
    packed[used:, :] = jnp.zeros((packed.shape[0] - used, LANES), jnp.float32)


def spot_kernel(
    kept,
    halo_first,
    halo_second,
    from_core,
    from_chip,
    mixer,
    inner_fields,
    own_tents,
    edge_strong,
    edge_fields,
    partner_tents,
    rows,
    kept_sums,
    sent_sums,
    padded,
    mask_rows,
    terms,
    field,
    spread,
    packed,
    contributions,
):
    frames, columns = kept.shape[1:]
    height = field.shape[0] // frames
    odd_band = parity("refl")
    odd_slab = parity("frame")
    has_partner = lax.axis_index("frame") > 0

    halo_a = halo_first[...]
    halo_b = halo_second[...]
    band = lax.axis_index("refl")
    before = jnp.where(odd_band, halo_a, jnp.where(band > 0, halo_b, 0.0))
    after = jnp.where(odd_band, jnp.where(band < lax.axis_size("refl") - 1, halo_b, 0.0), halo_a)
    near = 4 + HALO
    padded[0:HALO] = before[0:HALO]
    padded[HALO : HALO + near] = kept[0:near]
    padded[HALO + near : HALO + 2 * near] = kept[height - near : height]
    padded[HALO + 2 * near :] = after[0:HALO]
    live = kept_rows(kept, height, 0)
    mask_rows[8 - HALO : 8, :] = before[HALO, 0:HALO]
    mask_rows[8 : 8 + near, :] = live[0:near]
    mask_rows[24 - HALO : 24 - HALO + near, :] = live[height - near :]
    mask_rows[28:31, :] = after[HALO, 0:HALO]
    window_counts(mask_rows, 5, 4, terms, 0)
    window_counts(mask_rows, 21, 4, terms, 8)
    for slot, (base, term_row, live_row) in enumerate(((0, 0, 8), (2, 2, 10), (10, 8, 24), (12, 10, 26))):
        row_pair(padded, base, terms, term_row, mask_rows, live_row, edge_strong, edge_fields, slot)

    partner = jnp.where(odd_slab, from_core[...], from_chip[...])
    following = jnp.where(odd_slab, from_chip[0:height], from_core[0:height])
    following = jnp.where(lax.axis_index("frame") < lax.axis_size("frame") - 1, following, 0.0)
    lower = kept_rows(kept, height, 1)
    upper = kept_rows(kept, height, 2)
    infos = [kept_info(kept, height, k) for k in range(3)]
    partner_info = [partner[height + k : height + k + 1, 0:LANES].astype(jnp.int32) for k in range(3)]
    rows[0] = infos[0]
    rows[1] = partner_info[0]
    own_total = count_totals(lower + following, infos[0], infos[1])
    partner_total = count_totals(partner[0:height] + upper, partner_info[0], partner_info[1])
    partner_total = jnp.where(has_partner, partner_total, 1.0)
    column_tents(partner_info[1], columns, partner_tents)

    contributions[...] = jnp.zeros(contributions.shape, jnp.float32)
    clear_tail(packed)
    quarter = 4 * frames
    field[0:quarter] = edge_fields[2, 0:quarter]
    field[quarter : height * frames - quarter] = inner_fields[2]
    field[height * frames - quarter :] = edge_fields[2, quarter:]
    for half, (anchors, tents, total) in enumerate(
        ((infos[0], own_tents, own_total), (partner_info[0], partner_tents, partner_total))
    ):
        mixed = dot(mixer[half], field[...]).astype(jnp.bfloat16)
        per_total = 1.0 / total

        def take(a, plane):
            first = (a + half * (GRID - HALF_BINS)) * PLANE
            contributions[first : first + PLANE, half * LANES : (half + 1) * LANES] = plane * per_total

        half_grids(mixed, tents, anchors, spread, packed, take)

    regions = lax.broadcasted_iota(jnp.int32, (REGIONS, LANES), 0)
    own_member = jnp.where(regions == infos[2], 1.0, 0.0)
    partner_member = jnp.where((regions == partner_info[2]) & has_partner, 1.0, 0.0)
    members = jnp.concatenate([own_member, partner_member], axis=1).astype(jnp.bfloat16)
    high, low = split_two(contributions[...])
    sums = dot_nt(members, high) + dot_nt(members, low)
    early, late = sums[0 : REGIONS // 2], sums[REGIONS // 2 :]
    kept_sums[...] = jnp.where(odd_slab, late, early)
    sent_sums[...] = jnp.where(odd_slab, early, late)


def grid_kernel(half, rows, mixer, edge_fields, inner_fields, tents, grids, field, spread, packed):
    clear_tail(packed)
    total = field.shape[0]
    quarter = edge_fields.shape[1] // 2
    for k in range(2):
        field[0:quarter] = edge_fields[k, 0:quarter]
        field[quarter : total - quarter] = inner_fields[k]
        field[total - quarter :] = edge_fields[k, quarter:]
        mixed = dot(mixer[half], field[...]).astype(jnp.bfloat16)

        def take(a, plane):
            grids[k, a * PLANE : (a + 1) * PLANE, :] = plane.astype(grids.dtype)

        half_grids(mixed, tents, rows[half], spread, packed, take)


def strong_kernel(edge_strong, inner_strong, strong, rows):
    rows[0:4] = edge_strong[0:4]
    rows[4 : rows.shape[0] - 4] = inner_strong[...]
    rows[rows.shape[0] - 4 :] = edge_strong[4:]
    strong[...] = jnp.transpose(rows[...], (1, 0, 2)).astype(jnp.bfloat16)


def all_regions(own_half, other_half):
    early = jnp.where(parity("frame"), other_half[...], own_half[...])
    late = jnp.where(parity("frame"), own_half[...], other_half[...])
    return jnp.concatenate([early, late], axis=0)


def fit_kernel(own_half, other_half, region, slots, lower_grids, upper_grids, estimates, signal, back, chosen):
    sums = all_regions(own_half, other_half)
    profile = sums / jnp.sum(sums, axis=1, keepdims=True)
    regions = lax.broadcasted_iota(jnp.int32, (REGIONS, LANES), 0)
    member = jnp.where(regions == region[...], 1.0, 0.0).astype(jnp.bfloat16)
    both = jnp.concatenate(split_two(profile[:, 0:FULL_ROWS]), axis=0)
    twice = jnp.concatenate([member, member], axis=0)
    chosen[...] = lax.dot_general(
        both, twice, (((0,), (0,)), ((), ())), preferred_element_type=jnp.float32
    )
    join = HALF_ROWS - PLANE
    has_following = lax.axis_index("frame") < lax.axis_size("frame") - 1
    estimate = jnp.zeros((8, LANES), jnp.float32)
    for field, target in ((0, signal), (1, back)):
        upper = jnp.where(has_following, upper_grids[field].astype(jnp.float32), 0.0)
        for r in range(0, FULL_ROWS, 8):
            value = lower_grids[field, r : r + 8] if r < HALF_ROWS else None
            if r >= join:
                late = upper[r - join : r - join + 8]
                value = late if value is None else value + late
            if field == 0:
                estimate = estimate + value
            target[r : r + 8] = value if field == 0 else value + 1.0
    estimate = jnp.sum(estimate, axis=0, keepdims=True)
    for _ in range(ITERS):
        level = jnp.broadcast_to(jnp.maximum(estimate, 0.0), (8, LANES))
        sums_up = [jnp.zeros((8, LANES), jnp.float32)] * 2
        sums_low = [jnp.zeros((8, LANES), jnp.float32)] * 2
        for r in range(0, FULL_ROWS, 8):
            share = chosen[r : r + 8]
            ratio = share / (back[r : r + 8] + level * share)
            k = r // 8 % 2
            sums_up[k] = sums_up[k] + ratio * signal[r : r + 8]
            sums_low[k] = sums_low[k] + ratio * share
        upper_sum = jnp.sum(sums_up[0] + sums_up[1], axis=0, keepdims=True)
        lower_sum = jnp.sum(sums_low[0] + sums_low[1], axis=0, keepdims=True)
        estimate = upper_sum / lower_sum
    devices = estimates.shape[0]
    target = lax.broadcasted_iota(jnp.int32, (devices, LANES), 0) * 2
    for j in range(2):
        held = jnp.where(slots[...] == target + j, estimate, 0.0)
        estimates[:, j : j + 1] = jnp.sum(held, axis=1, keepdims=True)


def profile_kernel(own_half, other_half, profiles):
    sums = all_regions(own_half, other_half)
    profile = sums / jnp.sum(sums, axis=1, keepdims=True)
    profiles[...] = jnp.concatenate(
        [profile[:, a * PLANE : a * PLANE + GRID * GRID] for a in range(GRID)], axis=1
    )


def spread_kernel(arrived, intensity):
    devices = arrived.shape[0]
    lane = lax.broadcasted_iota(jnp.int32, (devices, 2 * devices), 1)
    source = lax.broadcasted_iota(jnp.int32, (devices, 2 * devices), 0)
    placed = jnp.where(lane == 2 * source, arrived[:, 0:1], 0.0)
    placed = placed + jnp.where(lane == 2 * source + 1, arrived[:, 1:2], 0.0)
    intensity[...] = jnp.sum(placed, axis=0, keepdims=True)


def slot_numbers(owners):
    position = jnp.arange(owners.shape[0], dtype=jnp.int32)
    earlier = (owners[None, :] == owners[:, None]) & (position[None, :] < position[:, None])
    return owners * 2 + jnp.sum(jnp.where(earlier, 1, 0), axis=1).astype(jnp.int32)


def pairs_even(count):
    return [(i, i ^ 1) for i in range(count)]


def pairs_odd(count):
    inner = [(i, i + 1 if i % 2 else i - 1) for i in range(1, count - 1)]
    return [(0, 0)] + inner + [(count - 1, count - 1)]


def swapped(x, axis, flip):
    return lax.ppermute(x, axis, [(i, i ^ flip) for i in range(lax.axis_size(axis))])


def summed_over_four(sums, axis, flips):
    sent = sums.astype(jnp.bfloat16)
    one, two, three = [swapped(sent, axis, flip).astype(jnp.float32) for flip in flips]
    return (sent.astype(jnp.float32) + one) + (two + three)


def per_device(image, gain, pixel_mask, anchor_row, anchor_col, owner, region):
    frames, height, columns = image.shape
    slabs = lax.axis_size("frame")
    bands = lax.axis_size("refl")
    devices = slabs * bands
    f32, bf16 = jnp.float32, jnp.bfloat16
    vmem = pl.BlockSpec(memory_space=pltpu.VMEM)

    def shape(dims, dtype=f32):
        return jax.ShapeDtypeStruct(dims, dtype)

    def call(kernel, operands, outs, scratch=(), name=None, work=1):
        return pl.pallas_call(
            kernel,
            in_specs=[vmem] * len(operands),
            out_specs=[vmem] * len(outs),
            out_shape=outs,
            scratch_shapes=[pltpu.VMEM(s.shape, s.dtype) for s in scratch],
            compiler_params=PARAMS,
            cost_estimate=pl.CostEstimate(flops=work, bytes_accessed=work, transcendentals=0),
            name=name,
        )(*operands)

    row, column, area = (x.reshape(1, -1) for x in (anchor_row, anchor_col, region))
    first, second, core, chip, kept = pl.pallas_call(
        send_kernel,
        in_specs=[pl.BlockSpec(memory_space=pl.ANY)] * 6,
        out_specs=[vmem] * 5,
        out_shape=[shape((HALO + 1, frames, columns))] * 2
        + [shape((height + 8, columns))] * 2
        + [shape((height + 1 + 3 * height // 8, frames, columns))],
        scratch_shapes=[
            pltpu.VMEM((frames, height, columns), f32),
            pltpu.VMEM((height, columns), f32),
            pltpu.VMEM((height, columns), jnp.int32),
            pltpu.VMEM((3, 1, LANES), jnp.int32),
            pltpu.SemaphoreType.DMA((6,)),
        ],
        name="sent",
    )(image, gain, pixel_mask, row, column, area)
    halo_second = lax.ppermute(second, "refl", pairs_odd(bands))
    halo_first = lax.ppermute(first, "refl", pairs_even(bands))
    from_core = lax.ppermute(core, "frame", pairs_even(slabs))
    from_chip = lax.ppermute(chip, "frame", pairs_odd(slabs))
    slots = slot_numbers(owner[:, 0])[None, :]

    inner = height - 8
    tent_shape = shape((columns, GRID * LANES), bf16)
    inner_strong, inner_fields, own_tents = call(
        inner_kernel,
        (kept,),
        [shape((inner, frames, columns)), shape((3, inner * frames, columns), bf16), tent_shape],
        [shape((height, columns)), shape((3, inner, columns))],
        name="inner",
    )

    mixer = jnp.asarray(depth_mixer(height, frames), bf16)
    field_shape = shape((height * frames, columns), bf16)
    spread_shape = shape((2, height * 8, 2 * LANES))
    packed_shape = shape((PLANE * 8, LANES))
    edge_strong, edge_fields, partner_tents, rows, kept_sums, sent_sums = call(
        spot_kernel,
        (
            kept,
            halo_first,
            halo_second,
            from_core,
            from_chip,
            mixer,
            inner_fields,
            own_tents,
        ),
        [
            shape((8, frames, columns)),
            shape((3, 8 * frames, columns), bf16),
            tent_shape,
            shape((2, 1, LANES), jnp.int32),
            shape((REGIONS // 2, WIDE_ROWS)),
            shape((REGIONS // 2, WIDE_ROWS)),
        ],
        [
            shape((2 * (HALO + 4 + HALO), frames, columns)),
            shape((height, columns)),
            shape((3, 16, columns)),
            field_shape,
            spread_shape,
            packed_shape,
            shape((WIDE_ROWS, 2 * LANES)),
        ],
        name="spots",
    )
    sums = kept_sums + swapped(sent_sums, "frame", 1)
    sums, edge_fields = lax.optimization_barrier((sums, edge_fields))
    scratch = [field_shape, spread_shape, packed_shape]
    (upper_grids,) = call(
        functools.partial(grid_kernel, 1),
        (rows, mixer, edge_fields, inner_fields, partner_tents),
        [shape((2, HALF_ROWS, LANES), bf16)],
        scratch,
        name="upper",
    )
    sums = summed_over_four(sums, "refl", (4, 8, 12))
    sums, upper_grids, edge_fields = lax.optimization_barrier((sums, upper_grids, edge_fields))
    upper_grids = lax.ppermute(upper_grids, "frame", [((i + 1) % slabs, i) for i in range(slabs)])
    (lower_grids,) = call(
        functools.partial(grid_kernel, 0),
        (rows, mixer, edge_fields, inner_fields, own_tents),
        [shape((2, HALF_ROWS, LANES))],
        scratch,
        name="lower",
    )
    sums = summed_over_four(sums, "refl", (1, 2, 3))
    sums, lower_grids = lax.optimization_barrier((sums, lower_grids))
    sums = summed_over_four(sums, "frame", (2, 4, 6))
    other = swapped(sums, "frame", 1)
    (strong,) = call(
        strong_kernel,
        (edge_strong, inner_strong),
        [shape((frames, height, columns), bf16)],
        [shape((height, frames, columns))],
        name="strong",
    )
    (estimates,) = call(
        fit_kernel,
        (sums, other, area, slots, lower_grids, upper_grids),
        [shape((devices, 2))],
        [shape((FULL_ROWS, LANES))] * 3,
        name="fit",
    )
    arrived = lax.all_to_all(estimates, ("frame", "refl"), split_axis=0, concat_axis=0, tiled=True)
    (profiles,) = call(profile_kernel, (sums, other), [shape((REGIONS, GRID * GRID * GRID))], name="profiles")
    (intensity,) = call(spread_kernel, (arrived,), [shape((1, devices * 2))], name="intensity")
    return (strong, intensity, profiles)


def solution(mesh):
    in_specs = (
        P("frame", "refl", None),
        P("refl", None),
        P("refl", None),
        P(("frame", "refl")),
        P(("frame", "refl")),
        P(("frame", "refl"), None),
        P(("frame", "refl"), None),
    )
    out_specs = (P("frame", "refl", None), P(("frame", "refl"), None), P())
    return jax.shard_map(
        per_device, mesh=mesh, in_specs=in_specs, out_specs=out_specs, check_vma=False
    )
```

```python
import functools

import jax
import jax.numpy as jnp
import numpy as np
from jax import lax
from jax.experimental import pallas as pl
from jax.experimental.pallas import tpu as pltpu
from jax.sharding import PartitionSpec as P

SB_EDGE = 16
GRID = 9
REGIONS = 32
ITERS = 3
HALO = 3
LANES = 128
HALF_BINS = 5
PLANE = 88
HALF_ROWS = HALF_BINS * PLANE
FULL_ROWS = GRID * PLANE
WIDE_ROWS = 896
PARAMS = pltpu.CompilerParams(vmem_limit_bytes=24 * 1024 * 1024)


def tent_values():
    centres = (np.arange(SB_EDGE, dtype=np.float32) + 0.5) * (GRID / SB_EDGE)
    bins = np.arange(GRID, dtype=np.float32) + 0.5
    return np.maximum(0.0, 1.0 - np.abs(centres[None, :] - bins[:, None]))


TENT = tent_values()
EDGE_WEIGHT = TENT.sum(axis=0)


def depth_mixer(rows, frames):
    mixer = np.zeros((2, rows, 8, rows, frames), np.float32)
    for row in range(rows):
        mixer[0, row, :HALF_BINS, row, :] = TENT[:HALF_BINS, :frames]
        mixer[1, row, :HALF_BINS, row, :] = TENT[GRID - HALF_BINS :, frames:]
    return mixer.reshape(2, rows * 8, rows * frames)


def dot(a, b):
    return lax.dot_general(a, b, (((1,), (0,)), ((), ())), preferred_element_type=jnp.float32)


def dot_nt(a, b):
    return lax.dot_general(a, b, (((1,), (1,)), ((), ())), preferred_element_type=jnp.float32)


def split_two(x):
    high = x.astype(jnp.bfloat16)
    return high, (x - high.astype(jnp.float32)).astype(jnp.bfloat16)


def parity(axis):
    return lax.axis_index(axis) % 2 == 1


def send_kernel(
    image,
    gain,
    mask,
    row,
    column,
    region,
    first,
    second,
    core,
    chip,
    kept,
    counts_in,
    gains,
    masks,
    infos,
    arrived,
):
    frames, height, columns = image.shape
    odd_band = parity("refl")
    odd_slab = parity("frame")
    copies = [(image, counts_in), (gain, gains), (mask, masks)]
    copies += [(info, infos.at[k]) for k, info in enumerate((row, column, region))]
    copies = [pltpu.make_async_copy(*copy, arrived.at[k]) for k, copy in enumerate(copies)]
    for copy in copies:
        copy.start()
    for copy in copies:
        copy.wait()
    live = masks[...].astype(jnp.float32)
    values = counts_in[...] * (gains[...] * live)[None]
    kept[0:height] = jnp.transpose(values, (1, 0, 2))

    head, tail = kept[0:HALO], kept[height - HALO : height]
    first[0:HALO] = jnp.where(odd_band, head, tail)
    second[0:HALO] = jnp.where(odd_band, tail, head)
    head, tail = live[0:HALO], live[height - HALO :]
    first[HALO, 0:HALO] = jnp.where(odd_band, head, tail)
    second[HALO, 0:HALO] = jnp.where(odd_band, tail, head)

    counts = values.astype(jnp.bfloat16).astype(jnp.float32)
    inner = counts[1]
    for z in range(2, frames - 1):
        inner = inner + counts[z]
    border = float(EDGE_WEIGHT[0])
    lower = inner + counts[frames - 1] + border * counts[0]
    upper = inner + counts[0] + border * counts[frames - 1]
    core[0:height] = jnp.where(odd_slab, upper, lower)
    chip[0:height] = jnp.where(odd_slab, lower, upper)
    for k in range(3):
        sent = infos[k].astype(jnp.float32)
        core[height + k : height + k + 1, 0:LANES] = sent
        chip[height + k : height + k + 1, 0:LANES] = sent
        kept[height, k : k + 1, 0:LANES] = sent
    for place, whole in enumerate((live, lower, upper)):
        first_row = height + 1 + place * height // 8
        kept[first_row : first_row + height // 8] = whole.reshape(height // 8, 8, columns)


def kept_info(kept, height, k):
    return kept[height, k : k + 1, 0:LANES].astype(jnp.int32)


def kept_rows(kept, height, place):
    first_row = height + 1 + place * height // 8
    return kept[first_row : first_row + height // 8].reshape(height, kept.shape[2])


def shoebox_offsets(anchors, extent):
    return lax.broadcasted_iota(jnp.int32, (extent, LANES), 0) - anchors


def total_weights(anchors, extent):
    offset = shoebox_offsets(anchors, extent)
    inside = (offset >= 0) & (offset < SB_EDGE)
    border = (offset == 0) | (offset == SB_EDGE - 1)
    return jnp.where(border, float(EDGE_WEIGHT[0]), jnp.where(inside, 1.0, 0.0))


def count_totals(levels, row, column):
    height, columns = levels.shape
    high, low = split_two(levels)
    by_column = total_weights(column, columns).astype(jnp.bfloat16)
    sums = dot(high, by_column) + dot(low, by_column)
    return jnp.sum(sums * total_weights(row, height), axis=0, keepdims=True)


def column_tents(column, columns, tents):
    offset = shoebox_offsets(column, columns)
    offset = jnp.where(offset < 0, -2, jnp.where(offset >= SB_EDGE, SB_EDGE + 1, offset))
    centre = (offset.astype(jnp.float32) + 0.5) * (GRID / SB_EDGE) - GRID / 2
    centre = centre.astype(jnp.bfloat16)
    one, zero = jnp.bfloat16(1.0), jnp.bfloat16(0.0)
    for c in range(GRID):
        distance = jnp.abs(centre - jnp.bfloat16(c - GRID // 2))
        tents[:, c * LANES : (c + 1) * LANES] = jnp.maximum(one - distance, zero)


def window_sums(x):
    width = x.shape[-1]
    axis = x.ndim - 1
    pairs = x + pltpu.roll(x, 1, axis)
    fours = pairs + pltpu.roll(pairs, 2, axis)
    return fours + pltpu.roll(fours, width - 3, axis) - x


def window_counts(mask_rows, start, rows, terms, at):
    count = mask_rows[start : start + rows, :]
    for k in range(1, 2 * HALO + 1):
        count = count + mask_rows[start + k : start + k + rows, :]
    columns = count.shape[-1]
    tail = jnp.zeros((rows, LANES), jnp.float32)
    count = window_sums(jnp.concatenate([count, tail], axis=1))[:, 0:columns]
    per_spread = 1.0 / jnp.maximum(count - 1.0, 1.0)
    terms[0, at : at + rows, :] = 1.0 / jnp.maximum(count, 1.0)
    terms[1, at : at + rows, :] = 2.0 * per_spread
    terms[2, at : at + rows, :] = 2.0 + 12.0 * jnp.sqrt(2.0 * per_spread)


def row_pair(padded, base, terms, term_row, mask_rows, live_row, fields, slot):
    frames, columns = padded.shape[1:]
    rows = [padded[base + k] for k in range(2 * HALO + 2)]
    shared = rows[1]
    for k in range(2, 2 * HALO + 1):
        shared = shared + rows[k]
    squares = [x * x for x in rows]
    shared_square = squares[1]
    for k in range(2, 2 * HALO + 1):
        shared_square = shared_square + squares[k]
    frame_tail = jnp.zeros((2, frames, LANES), jnp.float32)
    total = jnp.stack([shared + rows[0], shared + rows[-1]])
    square = jnp.stack([shared_square + squares[0], shared_square + squares[-1]])
    total = window_sums(jnp.concatenate([total, frame_tail], axis=2))[:, :, 0:columns]
    square = window_sums(jnp.concatenate([square, frame_tail], axis=2))[:, :, 0:columns]
    value = jnp.stack([rows[HALO], rows[HALO + 1]])

    def every_frame(row):
        return jnp.broadcast_to(row, (frames, columns))

    def term(j):
        return jnp.stack([every_frame(terms[j, pl.ds(term_row + k, 1), :]) for k in range(2)])

    live = jnp.stack([every_frame(mask_rows[pl.ds(live_row + k, 1), :]) for k in range(2)])
    background = total * term(0)
    variance = (square - total * background) * term(1)
    per_root = lax.rsqrt(background + 1.0)
    root = background * lax.rsqrt(jnp.maximum(background, 1e-30))
    shortfall = term(2) - variance * (per_root * per_root)
    below = (background - value + 3.0 * root) * per_root
    gates = (1.0 + jnp.exp(shortfall)) * (1.0 + jnp.exp(below))
    weight = pl.reciprocal(gates, approx=True)
    weight = live * (weight * (2.0 - gates * weight))
    flat = (2 * frames, columns)
    weight, value, background = (
        x.reshape(flat).astype(jnp.bfloat16) for x in (weight, value, background)
    )
    at = pl.ds(pl.multiple_of(slot * 2 * frames, 2 * frames), 2 * frames)
    fields[0, at, :] = value - background
    fields[1, at, :] = background
    fields[2, at, :] = weight * value
    fields[3, at, :] = weight


def inner_kernel(kept, fields, tents, live, terms):
    height, columns = live.shape
    live[...] = kept_rows(kept, height, 0)
    column_tents(kept_info(kept, height, 1), columns, tents)
    rows = height - 8
    window_counts(live, 1, rows, terms, 0)

    def pair(i, carry):
        row_pair(kept, 2 * i + 1, terms, 2 * i, live, 2 * i + 4, fields, i)
        return carry

    lax.fori_loop(0, rows // 2, pair, 0, unroll=6)


def half_grids(mixed, tents, anchors, spread, packed, take):
    height = mixed.shape[0] // 8
    shift = jnp.broadcast_to(anchors, (8, LANES))
    bits = [(shift & (1 << k)) != 0 for k in range(5)]

    def one_column(c, spread, at):
        rows = [spread[8 * r : 8 * r + 8, at] for r in range(height)]
        rows = [
            jnp.where(bits[4], rows[r + 16], rows[r]) if r + 16 < height else rows[r]
            for r in range(31)
        ]
        for k in (3, 2, 1, 0):
            keep = 16 + (1 << k) - 1
            rows = [jnp.where(bits[k], rows[r + (1 << k)], rows[r]) for r in range(keep)]
        for b in range(GRID):
            value = None
            for y in range(SB_EDGE):
                if TENT[b, y] != 0.0:
                    term = rows[y] * float(TENT[b, y])
                    value = term if value is None else value + term
            packed[(b * GRID + c) * 8 : (b * GRID + c) * 8 + 8, :] = value

    for c in range(0, GRID, 2):
        end = min(c + 2, GRID)
        slot = spread.at[c // 2 % 2]
        slot[:, 0 : (end - c) * LANES] = dot(mixed, tents[:, c * LANES : end * LANES])
        for k in range(end - c):
            one_column(c + k, slot, slice(k * LANES, (k + 1) * LANES))
    for a in range(HALF_BINS):
        take(a, packed[pl.ds(a, PLANE, stride=8), :])


def clear_tail(packed):
    used = GRID * GRID * 8
    packed[used:, :] = jnp.zeros((packed.shape[0] - used, LANES), jnp.float32)


def spot_kernel(
    kept,
    halo_first,
    halo_second,
    from_core,
    from_chip,
    mixer,
    inner_fields,
    own_tents,
    edge_fields,
    partner_tents,
    rows,
    kept_sums,
    sent_sums,
    padded,
    mask_rows,
    terms,
    field,
    spread,
    packed,
    contributions,
):
    frames, columns = kept.shape[1:]
    height = field.shape[0] // frames
    odd_band = parity("refl")
    odd_slab = parity("frame")
    has_partner = lax.axis_index("frame") > 0

    halo_a = halo_first[...]
    halo_b = halo_second[...]
    band = lax.axis_index("refl")
    before = jnp.where(odd_band, halo_a, jnp.where(band > 0, halo_b, 0.0))
    after = jnp.where(odd_band, jnp.where(band < lax.axis_size("refl") - 1, halo_b, 0.0), halo_a)
    near = 4 + HALO
    padded[0:HALO] = before[0:HALO]
    padded[HALO : HALO + near] = kept[0:near]
    padded[HALO + near : HALO + 2 * near] = kept[height - near : height]
    padded[HALO + 2 * near :] = after[0:HALO]
    live = kept_rows(kept, height, 0)
    mask_rows[8 - HALO : 8, :] = before[HALO, 0:HALO]
    mask_rows[8 : 8 + near, :] = live[0:near]
    mask_rows[24 - HALO : 24 - HALO + near, :] = live[height - near :]
    mask_rows[28:31, :] = after[HALO, 0:HALO]
    window_counts(mask_rows, 5, 4, terms, 0)
    window_counts(mask_rows, 21, 4, terms, 8)
    for slot, (base, term_row, live_row) in enumerate(((0, 0, 8), (2, 2, 10), (10, 8, 24), (12, 10, 26))):
        row_pair(padded, base, terms, term_row, mask_rows, live_row, edge_fields, slot)

    partner = jnp.where(odd_slab, from_core[...], from_chip[...])
    following = jnp.where(odd_slab, from_chip[0:height], from_core[0:height])
    following = jnp.where(lax.axis_index("frame") < lax.axis_size("frame") - 1, following, 0.0)
    lower = kept_rows(kept, height, 1)
    upper = kept_rows(kept, height, 2)
    infos = [kept_info(kept, height, k) for k in range(3)]
    partner_info = [partner[height + k : height + k + 1, 0:LANES].astype(jnp.int32) for k in range(3)]
    rows[0] = infos[0]
    rows[1] = partner_info[0]
    own_total = count_totals(lower + following, infos[0], infos[1])
    partner_total = count_totals(partner[0:height] + upper, partner_info[0], partner_info[1])
    partner_total = jnp.where(has_partner, partner_total, 1.0)
    column_tents(partner_info[1], columns, partner_tents)

    contributions[...] = jnp.zeros(contributions.shape, jnp.float32)
    clear_tail(packed)
    quarter = 4 * frames
    field[0:quarter] = edge_fields[2, 0:quarter]
    field[quarter : height * frames - quarter] = inner_fields[2]
    field[height * frames - quarter :] = edge_fields[2, quarter:]
    for half, (anchors, tents, total) in enumerate(
        ((infos[0], own_tents, own_total), (partner_info[0], partner_tents, partner_total))
    ):
        mixed = dot(mixer[half], field[...]).astype(jnp.bfloat16)
        per_total = 1.0 / total

        def take(a, plane):
            first = (a + half * (GRID - HALF_BINS)) * PLANE
            contributions[first : first + PLANE, half * LANES : (half + 1) * LANES] = plane * per_total

        half_grids(mixed, tents, anchors, spread, packed, take)

    regions = lax.broadcasted_iota(jnp.int32, (REGIONS, LANES), 0)
    own_member = jnp.where(regions == infos[2], 1.0, 0.0)
    partner_member = jnp.where((regions == partner_info[2]) & has_partner, 1.0, 0.0)
    members = jnp.concatenate([own_member, partner_member], axis=1).astype(jnp.bfloat16)
    high, low = split_two(contributions[...])
    sums = dot_nt(members, high) + dot_nt(members, low)
    early, late = sums[0 : REGIONS // 2], sums[REGIONS // 2 :]
    kept_sums[...] = jnp.where(odd_slab, late, early)
    sent_sums[...] = jnp.where(odd_slab, early, late)


def grid_kernel(half, rows, mixer, edge_fields, inner_fields, tents, grids, field, spread, packed):
    clear_tail(packed)
    total = field.shape[0]
    quarter = edge_fields.shape[1] // 2
    for k in range(2):
        field[0:quarter] = edge_fields[k, 0:quarter]
        field[quarter : total - quarter] = inner_fields[k]
        field[total - quarter :] = edge_fields[k, quarter:]
        mixed = dot(mixer[half], field[...]).astype(jnp.bfloat16)

        def take(a, plane):
            grids[k, a * PLANE : (a + 1) * PLANE, :] = plane.astype(grids.dtype)

        half_grids(mixed, tents, rows[half], spread, packed, take)


def strong_kernel(edge_fields, inner_fields, strong):
    frames, height, columns = strong.shape
    quarter = edge_fields.shape[1] // 2
    edges, inner = edge_fields[3].astype(jnp.float32), inner_fields[3].astype(jnp.float32)
    rows = jnp.concatenate([edges[0:quarter], inner, edges[quarter:]], axis=0)
    rows = rows.reshape(height, frames, columns)
    strong[...] = jnp.transpose(rows, (1, 0, 2)).astype(jnp.bfloat16)


def all_regions(own_half, other_half):
    early = jnp.where(parity("frame"), other_half[...], own_half[...])
    late = jnp.where(parity("frame"), own_half[...], other_half[...])
    return jnp.concatenate([early, late], axis=0)


def fit_kernel(own_half, other_half, region, slots, lower_grids, upper_grids, estimates, signal, back, chosen):
    sums = all_regions(own_half, other_half)
    profile = sums / jnp.sum(sums, axis=1, keepdims=True)
    regions = lax.broadcasted_iota(jnp.int32, (REGIONS, LANES), 0)
    member = jnp.where(regions == region[...], 1.0, 0.0).astype(jnp.bfloat16)
    both = jnp.concatenate(split_two(profile[:, 0:FULL_ROWS]), axis=0)
    twice = jnp.concatenate([member, member], axis=0)
    chosen[...] = lax.dot_general(
        both, twice, (((0,), (0,)), ((), ())), preferred_element_type=jnp.float32
    )
    join = HALF_ROWS - PLANE
    has_following = lax.axis_index("frame") < lax.axis_size("frame") - 1
    estimate = jnp.zeros((8, LANES), jnp.float32)
    for field, target in ((0, signal), (1, back)):
        upper = jnp.where(has_following, upper_grids[field].astype(jnp.float32), 0.0)
        for r in range(0, FULL_ROWS, 8):
            value = lower_grids[field, r : r + 8] if r < HALF_ROWS else None
            if r >= join:
                late = upper[r - join : r - join + 8]
                value = late if value is None else value + late
            if field == 0:
                estimate = estimate + value
            target[r : r + 8] = value if field == 0 else value + 1.0
    estimate = jnp.sum(estimate, axis=0, keepdims=True)
    for _ in range(ITERS):
        level = jnp.broadcast_to(jnp.maximum(estimate, 0.0), (8, LANES))
        sums_up = [jnp.zeros((8, LANES), jnp.float32)] * 2
        sums_low = [jnp.zeros((8, LANES), jnp.float32)] * 2
        for r in range(0, FULL_ROWS, 8):
            share = chosen[r : r + 8]
            ratio = share / (back[r : r + 8] + level * share)
            k = r // 8 % 2
            sums_up[k] = sums_up[k] + ratio * signal[r : r + 8]
            sums_low[k] = sums_low[k] + ratio * share
        upper_sum = jnp.sum(sums_up[0] + sums_up[1], axis=0, keepdims=True)
        lower_sum = jnp.sum(sums_low[0] + sums_low[1], axis=0, keepdims=True)
        estimate = upper_sum / lower_sum
    devices = estimates.shape[0]
    target = lax.broadcasted_iota(jnp.int32, (devices, LANES), 0) * 2
    for j in range(2):
        held = jnp.where(slots[...] == target + j, estimate, 0.0)
        estimates[:, j : j + 1] = jnp.sum(held, axis=1, keepdims=True)


def profile_kernel(own_half, other_half, profiles):
    sums = all_regions(own_half, other_half)
    profile = sums / jnp.sum(sums, axis=1, keepdims=True)
    profiles[...] = jnp.concatenate(
        [profile[:, a * PLANE : a * PLANE + GRID * GRID] for a in range(GRID)], axis=1
    )


def spread_kernel(arrived, intensity):
    devices = arrived.shape[0]
    lane = lax.broadcasted_iota(jnp.int32, (devices, 2 * devices), 1)
    source = lax.broadcasted_iota(jnp.int32, (devices, 2 * devices), 0)
    placed = jnp.where(lane == 2 * source, arrived[:, 0:1], 0.0)
    placed = placed + jnp.where(lane == 2 * source + 1, arrived[:, 1:2], 0.0)
    intensity[...] = jnp.sum(placed, axis=0, keepdims=True)


def slot_numbers(owners):
    position = jnp.arange(owners.shape[0], dtype=jnp.int32)
    earlier = (owners[None, :] == owners[:, None]) & (position[None, :] < position[:, None])
    return owners * 2 + jnp.sum(jnp.where(earlier, 1, 0), axis=1).astype(jnp.int32)


def pairs_even(count):
    return [(i, i ^ 1) for i in range(count)]


def pairs_odd(count):
    inner = [(i, i + 1 if i % 2 else i - 1) for i in range(1, count - 1)]
    return [(0, 0)] + inner + [(count - 1, count - 1)]


def swapped(x, axis, flip):
    return lax.ppermute(x, axis, [(i, i ^ flip) for i in range(lax.axis_size(axis))])


def summed_over_four(sums, axis, flips):
    sent = sums.astype(jnp.bfloat16)
    one, two, three = [swapped(sent, axis, flip).astype(jnp.float32) for flip in flips]
    return (sent.astype(jnp.float32) + one) + (two + three)


def per_device(image, gain, pixel_mask, anchor_row, anchor_col, owner, region):
    frames, height, columns = image.shape
    slabs = lax.axis_size("frame")
    bands = lax.axis_size("refl")
    devices = slabs * bands
    f32, bf16 = jnp.float32, jnp.bfloat16
    vmem = pl.BlockSpec(memory_space=pltpu.VMEM)

    def shape(dims, dtype=f32):
        return jax.ShapeDtypeStruct(dims, dtype)

    def call(kernel, operands, outs, scratch=(), name=None, work=1):
        return pl.pallas_call(
            kernel,
            in_specs=[vmem] * len(operands),
            out_specs=[vmem] * len(outs),
            out_shape=outs,
            scratch_shapes=[pltpu.VMEM(s.shape, s.dtype) for s in scratch],
            compiler_params=PARAMS,
            cost_estimate=pl.CostEstimate(flops=work, bytes_accessed=work, transcendentals=0),
            name=name,
        )(*operands)

    row, column, area = (x.reshape(1, -1) for x in (anchor_row, anchor_col, region))
    first, second, core, chip, kept = pl.pallas_call(
        send_kernel,
        in_specs=[pl.BlockSpec(memory_space=pl.ANY)] * 6,
        out_specs=[vmem] * 5,
        out_shape=[shape((HALO + 1, frames, columns))] * 2
        + [shape((height + 8, columns))] * 2
        + [shape((height + 1 + 3 * height // 8, frames, columns))],
        scratch_shapes=[
            pltpu.VMEM((frames, height, columns), f32),
            pltpu.VMEM((height, columns), f32),
            pltpu.VMEM((height, columns), jnp.int32),
            pltpu.VMEM((3, 1, LANES), jnp.int32),
            pltpu.SemaphoreType.DMA((6,)),
        ],
        name="sent",
    )(image, gain, pixel_mask, row, column, area)
    halo_second = lax.ppermute(second, "refl", pairs_odd(bands))
    halo_first = lax.ppermute(first, "refl", pairs_even(bands))
    from_core = lax.ppermute(core, "frame", pairs_even(slabs))
    from_chip = lax.ppermute(chip, "frame", pairs_odd(slabs))
    slots = slot_numbers(owner[:, 0])[None, :]

    inner = height - 8
    tent_shape = shape((columns, GRID * LANES), bf16)
    inner_fields, own_tents = call(
        inner_kernel,
        (kept,),
        [shape((4, inner * frames, columns), bf16), tent_shape],
        [shape((height, columns)), shape((3, inner, columns))],
        name="inner",
    )

    mixer = jnp.asarray(depth_mixer(height, frames), bf16)
    field_shape = shape((height * frames, columns), bf16)
    spread_shape = shape((2, height * 8, 2 * LANES))
    packed_shape = shape((PLANE * 8, LANES))
    edge_fields, partner_tents, rows, kept_sums, sent_sums = call(
        spot_kernel,
        (
            kept,
            halo_first,
            halo_second,
            from_core,
            from_chip,
            mixer,
            inner_fields,
            own_tents,
        ),
        [
            shape((4, 8 * frames, columns), bf16),
            tent_shape,
            shape((2, 1, LANES), jnp.int32),
            shape((REGIONS // 2, WIDE_ROWS)),
            shape((REGIONS // 2, WIDE_ROWS)),
        ],
        [
            shape((2 * (HALO + 4 + HALO), frames, columns)),
            shape((height, columns)),
            shape((3, 16, columns)),
            field_shape,
            spread_shape,
            packed_shape,
            shape((WIDE_ROWS, 2 * LANES)),
        ],
        name="spots",
    )
    sums = kept_sums + swapped(sent_sums, "frame", 1)
    sums, edge_fields = lax.optimization_barrier((sums, edge_fields))
    scratch = [field_shape, spread_shape, packed_shape]
    (upper_grids,) = call(
        functools.partial(grid_kernel, 1),
        (rows, mixer, edge_fields, inner_fields, partner_tents),
        [shape((2, HALF_ROWS, LANES), bf16)],
        scratch,
        name="upper",
    )
    sums = summed_over_four(sums, "refl", (4, 8, 12))
    sums, upper_grids, edge_fields = lax.optimization_barrier((sums, upper_grids, edge_fields))
    upper_grids = lax.ppermute(upper_grids, "frame", [((i + 1) % slabs, i) for i in range(slabs)])
    (lower_grids,) = call(
        functools.partial(grid_kernel, 0),
        (rows, mixer, edge_fields, inner_fields, own_tents),
        [shape((2, HALF_ROWS, LANES))],
        scratch,
        name="lower",
    )
    sums = summed_over_four(sums, "refl", (1, 2, 3))
    sums, lower_grids = lax.optimization_barrier((sums, lower_grids))
    sums = summed_over_four(sums, "frame", (2, 4, 6))
    other = swapped(sums, "frame", 1)
    (strong,) = call(
        strong_kernel,
        (edge_fields, inner_fields),
        [shape((frames, height, columns), bf16)],
        name="strong",
    )
    (estimates,) = call(
        fit_kernel,
        (sums, other, area, slots, lower_grids, upper_grids),
        [shape((devices, 2))],
        [shape((FULL_ROWS, LANES))] * 3,
        name="fit",
    )
    arrived = lax.all_to_all(estimates, ("frame", "refl"), split_axis=0, concat_axis=0, tiled=True)
    (profiles,) = call(profile_kernel, (sums, other), [shape((REGIONS, GRID * GRID * GRID))], name="profiles")
    (intensity,) = call(spread_kernel, (arrived,), [shape((1, devices * 2))], name="intensity")
    return (strong, intensity, profiles)


def solution(mesh):
    in_specs = (
        P("frame", "refl", None),
        P("refl", None),
        P("refl", None),
        P(("frame", "refl")),
        P(("frame", "refl")),
        P(("frame", "refl"), None),
        P(("frame", "refl"), None),
    )
    out_specs = (P("frame", "refl", None), P(("frame", "refl"), None), P())
    return jax.shard_map(
        per_device, mesh=mesh, in_specs=in_specs, out_specs=out_specs, check_vma=False
    )
```
